32 devices in a mesh: groups: 2 (over y), rank: 16 (over z, x, core).
Axes of the slice: x: 2, y: 2, z: 4, core: 2. Of those that a mesh axis runs over, the one named last changes fastest.
Arguments:
- pool: bfloat16 [512, 1024], P(('groups', 'rank')), parts along dimension 0, may hold values from -6 to 6
- kv_cache: bfloat16 [128, 4, 64, 256], P(('groups', 'rank')), parts along dimension 0
- w_qu: bfloat16 [1024, 1024], replicated, may hold values from -0.1875 to 0.1875
- w_out: bfloat16 [512, 1024], replicated, may hold values from -0.25 to 0.25
- norm_gain: float32 [512], replicated, may hold values from 0.1 to 1.9
- cand_ids: int32 [8, 2048], P('groups'), parts along dimension 0, may hold values from 0 to 255
- ranker: int32 [4], replicated, may hold values from 0 to 3, each once
- hist_blocks: int32 [8], P('groups'), parts along dimension 0, may hold values from 4 to 16, as said below
- cache_slot: int32 [8, 16], P('groups'), parts along dimension 0, may hold values from 0 to 63, as said below
Outputs:
- ranked: bfloat16 [16384, 1024], P(('groups', 'rank')), parts along dimension 0
The draws below stay inside these ranges and needn't reach their ends.
There are 2 independent parts, one for each index of `groups`. The reference program is written for one: setup_inputs(seed, part) draws one part's arguments, and reference() takes and returns one part's arrays. A program takes and returns all parts, laid end to end along the dimension named above; an argument that names none is the same for every part. Nothing has to cross between parts.
Inputs may be any that keep to these rules, and one draw needn't show every extreme that they name: Block b of user u (b < 16) is held in slot cache_slot[u, b], which lies on device cache_slot[u, b] // 4 of the rank axis. Each slot holds exactly one pair (u, b); the 16 blocks of one user lie on 16 different devices. `ranker`: each ranking group scores exactly one user. User u's history is its blocks 0 to hist_blocks[u] - 1; its other blocks are unused. Some user has 16 blocks.
All inputs are finite; a program needn't handle non-finite values.
Results may differ from the reference program's by a relative error of at most 0.0054.
Values may be sent and summed in bfloat16 or wider, within the bound.
A program may use at most 128 MiB of HBM per device.

```python
import jax
import jax.numpy as jnp
from jax import lax

D = 1024
HEADS = 4
HEAD_DIM = 128
BLOCK = 64
CAND = 2048
HB = 16
USERS = 4
BLK_DEV = 4
SLOTS = 64
POOL = 256
N_RANK = 16


def draw_cache_slot(key, part):
    key_order, key_turn, key_owner = jax.random.split(jax.random.fold_in(key, 11), 3)
    user_order = jax.random.permutation(key_order, USERS)
    user_class = user_order // BLK_DEV
    slot_place = user_order % BLK_DEV
    rotation = jax.random.randint(key_turn, (USERS,), 0, HB)
    owner_order = jax.random.permutation(key_owner, N_RANK)
    position = user_class[:, None] * HB + (jnp.arange(HB)[None, :] + rotation[:, None]) % HB
    owners = owner_order[position]
    return (owners * BLK_DEV + slot_place[:, None]).astype(jnp.int32)


def draw_hist_blocks(key, part):
    key_length, key_pick = jax.random.split(jax.random.fold_in(key, 23))
    lengths = jax.random.randint(key_length, (USERS,), HB // 4, HB + 1)
    chosen = jax.random.permutation(key_pick, USERS)
    lengths = lengths.at[chosen[0]].set(HB).at[chosen[1]].set(HB // 4)
    return lengths.astype(jnp.int32)


def draw_kv_cache(key, part):
    key_base, key_column = jax.random.split(jax.random.fold_in(key, 37))
    array_shape = (SLOTS, HEADS, BLOCK, 2 * HEAD_DIM)
    column_draw = jax.random.uniform(key_column, (HEADS, 2 * HEAD_DIM), jnp.float32)
    head_place = jnp.arange(HEADS, dtype=jnp.float32) / (HEADS - 1)
    is_value = jnp.arange(2 * HEAD_DIM) >= HEAD_DIM
    base_draw = jax.random.normal(key_base, array_shape, jnp.float32)
    key_scale = 0.5 * 4.0 ** column_draw
    value_scale = 10.0 ** column_draw * (2.0 ** head_place)[:, None]
    factor = jnp.where(is_value[None, :], value_scale, key_scale)
    return (base_draw * factor[None, :, None, :]).astype(jnp.bfloat16)


def with_ends(array, stream_key, low, largest):
    index_at = [jax.random.randint(jax.random.fold_in(stream_key, axis), (), 0, length) for axis, length in enumerate(array.shape)]
    main_axis = array.shape.index(max(array.shape))
    next_to = index_at[:main_axis] + [(index_at[main_axis] + 1) % array.shape[main_axis]] + index_at[main_axis + 1:]
    return array.at[tuple(index_at)].set(low).at[tuple(next_to)].set(largest)


def level_of(own_key, dims, cuts, least, high):
    gain = 1.0
    for axis_at, shards_of in cuts:
        steps = jax.random.uniform(jax.random.fold_in(jax.random.fold_in(own_key, 6), axis_at), (shards_of,), jnp.float32, least / len(cuts), high / len(cuts))
        gain = gain * jnp.repeat(jnp.exp(steps), dims[axis_at] // shards_of).reshape((-1,) + (1,) * (len(dims) - 1 - axis_at))
    return gain


def normal_values(stream_key, shape, spread, most, cuts=(), kind=jnp.bfloat16):
    loudness = level_of(stream_key, shape, cuts, -0.22, 0.18) if cuts else 1.0
    array = jax.random.normal(stream_key, shape, jnp.float32) * spread * loudness
    return jnp.minimum(jnp.maximum(array, -most), most).astype(kind)


def setup_inputs(seed: int = 0, part: int = 0) -> dict:
    key_of = jax.random.split(jax.random.key(seed), 10)
    part_keys = jax.random.split(jax.random.fold_in(key_of[9], part), 10)
    return {
        "pool": normal_values(part_keys[0], (POOL, D), 1.0, 6.0, ((0, 16),)),
        "kv_cache": draw_kv_cache(jax.random.fold_in(jax.random.fold_in(key_of[9], part), 71), part),
        "w_qu": normal_values(key_of[2], (D, HEADS * 2 * HEAD_DIM), D ** -0.5, 0.1875),
        "w_out": normal_values(key_of[3], (HEADS * HEAD_DIM, D), (HEADS * HEAD_DIM) ** -0.5, 0.25),
        "norm_gain": jnp.clip(1.0 + 0.18 * jax.random.normal(key_of[4], (HEADS * HEAD_DIM,), jnp.float32), 0.1, 1.9),
        "cand_ids": with_ends(jax.random.randint(part_keys[5], (USERS, CAND), 0, POOL), jax.random.fold_in(part_keys[5], 1), 0, POOL - 1).astype(jnp.int32),
        "ranker": jax.random.permutation(key_of[6], USERS).astype(jnp.int32),
        "hist_blocks": draw_hist_blocks(jax.random.fold_in(jax.random.fold_in(key_of[9], part), 71), part),
        "cache_slot": draw_cache_slot(jax.random.fold_in(jax.random.fold_in(key_of[9], part), 71), part),
    }


norm_eps = 1e-05

def reference(pool, kv_cache, w_qu, w_out, norm_gain, cand_ids, ranker, hist_blocks, cache_slot):
    user_count = ranker.shape[0]
    user_range = jnp.arange(user_count, dtype=jnp.int32)
    user_of_group = jnp.zeros((user_count,), jnp.int32).at[ranker].set(user_range)
    score_scale = 1.0 / HEAD_DIM ** 0.5

    def one_user(user_index):
        cand_rows = jnp.take(pool, cand_ids[user_index], axis=0)
        head_qu = jax.nn.silu(jnp.dot(cand_rows, w_qu, preferred_element_type=jnp.float32)).astype(jnp.bfloat16)
        head_qu = head_qu.reshape(CAND, HEADS, 2, HEAD_DIM).astype(jnp.float32)
        queries = head_qu[:, :, 0, :]
        gates = head_qu[:, :, 1, :].reshape(CAND, HEADS * HEAD_DIM)
        history = jnp.take(kv_cache, cache_slot[user_index], axis=0)
        live_blocks = jnp.arange(HB) < hist_blocks[user_index]
        history = jnp.where(live_blocks[:, None, None, None], history, jnp.zeros_like(history))
        history = jnp.transpose(history, (1, 0, 2, 3)).reshape(HEADS, HB * BLOCK, 2 * HEAD_DIM).astype(jnp.float32)
        scores = jnp.einsum('chd,hkd->hck', queries, history[:, :, :HEAD_DIM])
        weights = jax.nn.silu(scores * score_scale).astype(jnp.bfloat16)
        weights = lax.optimization_barrier(weights).astype(jnp.float32)
        attended = jnp.einsum('hck,hkd->chd', weights, history[:, :, HEAD_DIM:]).reshape(CAND, HEADS * HEAD_DIM)
        mean_value = lax.optimization_barrier(jnp.mean(attended, axis=1, keepdims=True))
        variance = lax.optimization_barrier(jnp.mean(attended * attended, axis=1, keepdims=True)) - mean_value * mean_value
        hidden = ((attended - mean_value) * lax.rsqrt(variance + norm_eps) * norm_gain[None, :] * gates).astype(jnp.bfloat16)
        mixed = cand_rows.astype(jnp.float32) + jnp.dot(hidden, w_out, preferred_element_type=jnp.float32)
        return mixed.astype(jnp.bfloat16)
    results = lax.map(one_user, user_of_group)
    return results.reshape(USERS * CAND, D)
```

```python
import functools
import math

import jax
import jax.numpy as jnp
from jax import lax
from jax.experimental import pallas as pl
from jax.experimental.pallas import tpu as pltpu
from jax.sharding import PartitionSpec as P

norm_eps = 1e-05
MESH = pl.DeviceIdType.MESH


def partner(shard, axis, bit):
    return lax.ppermute(shard, axis, [(i, i ^ 1 << bit) for i in range(lax.axis_size(axis))])


def attend_blocks(queries, stacked, head_dim, live_steps):
    score_scale = 1.0 / math.sqrt(head_dim)

    def step_fn(running, item):
        step_index, key_block = item

        def compute(total):
            key_part = key_block[:, :head_dim]
            value_part = key_block[:, head_dim:]
            scores = lax.dot_general(
                queries, key_part, (((1,), (1,)), ((), ())), preferred_element_type=jnp.float32
            )
            weights = jax.nn.silu(scores * score_scale).astype(jnp.bfloat16)
            return total + jnp.dot(weights, value_part, preferred_element_type=jnp.float32)

        def keep_same(total):
            return total

        return (lax.cond(step_index < live_steps, compute, keep_same, running), None)

    initial = jnp.zeros((queries.shape[0], head_dim), jnp.float32)
    step_ids = jnp.arange(stacked.shape[0], dtype=jnp.int32)
    attended, unused = lax.scan(step_fn, initial, (step_ids, stacked))
    return attended


def candidate_body(pool, kv_cache, w_qu, w_out, norm_gain, cand_ids, ranker, hist_blocks, cache_slot):
    devices = lax.axis_size("rank")
    my_index = lax.axis_index("rank")
    slots_here, head_count, block_len, pair_width = kv_cache.shape
    head_dim = pair_width // 2
    user_count, most_blocks = cache_slot.shape
    model_width = pool.shape[1]
    cand_count = cand_ids.shape[1]
    slice_width = model_width // head_count
    qu_cols = 2 * head_dim
    my_group = my_index // head_count
    my_head = my_index % head_count
    bit_count = head_count.bit_length() - 1
    share_rows = cand_count // head_count
    user_range = jnp.arange(user_count, dtype=jnp.int32)
    group_match = ranker[None, :] == user_range[:, None]
    user_of_group = jnp.sum(jnp.where(group_match, user_range[None, :], 0), axis=1)
    my_user = jnp.sum(jnp.where(user_range == my_group, user_of_group, 0))
    block_range = jnp.arange(most_blocks, dtype=jnp.int32)
    live_blocks = block_range[None, :] < hist_blocks[:, None]
    owner_table = cache_slot // slots_here
    held_here = live_blocks & (owner_table == my_index)
    held_slot = jnp.sum(jnp.where(held_here, cache_slot % slots_here, 0), axis=1)
    held_flag = jnp.any(held_here, axis=1)
    slot_of_group = jnp.sum(jnp.where(group_match, held_slot[None, :], 0), axis=1)
    flag_of_group = jnp.any(group_match & held_flag[None, :], axis=1)
    outgoing = jnp.take(kv_cache, slot_of_group, axis=0)
    outgoing = jnp.where(flag_of_group[:, None, None, None], outgoing, jnp.zeros_like(outgoing))
    outgoing = outgoing.reshape(devices, block_len, pair_width)
    incoming = lax.all_to_all(outgoing, "rank", split_axis=0, concat_axis=0, tiled=True)
    my_ids = lax.dynamic_index_in_dim(cand_ids, my_user, 0, keepdims=False)
    whole_pool = lax.all_gather(pool, "rank", axis=0, tiled=True)
    cand_rows = jnp.take(whole_pool, my_ids, axis=0)
    w_head = lax.dynamic_slice_in_dim(w_qu, my_head * qu_cols, qu_cols, 1)
    head_qu = jax.nn.silu(jnp.dot(cand_rows, w_head, preferred_element_type=jnp.float32)).astype(
        jnp.bfloat16
    )
    x_part = lax.dynamic_slice_in_dim(cand_rows, my_head * slice_width, slice_width, 1)
    queries = head_qu[:, :head_dim]
    gate_part = head_qu[:, head_dim:]
    step_sources = min(16, devices)
    stacked = incoming.reshape(devices // step_sources, step_sources * block_len, pair_width)
    live_steps = stacked.shape[0]
    attended = attend_blocks(queries, stacked, head_dim, live_steps)
    total_width = head_count * head_dim
    carried = jnp.concatenate(
        [attended, gate_part.astype(jnp.float32), x_part.astype(jnp.float32)], axis=1
    )
    state = carried.reshape(head_count, share_rows, 1, carried.shape[1])
    for bit_index in reversed(range(bit_count)):
        half_count = state.shape[0] // 2
        lower_half = state[:half_count]
        upper_half = state[half_count:]
        upper_side = my_head >> bit_index & 1 == 1
        keeping = jnp.where(upper_side, upper_half, lower_half)
        giving = jnp.where(upper_side, lower_half, upper_half)
        received = partner(giving, "rank", bit_index)
        state = jnp.where(
            upper_side,
            jnp.concatenate([received, keeping], axis=2),
            jnp.concatenate([keeping, received], axis=2),
        )
    reversal = [
        sum(((source >> bit & 1) << bit_count - 1 - bit for bit in range(bit_count)))
        for source in range(head_count)
    ]
    ordered = state[0][:, jnp.array(reversal, dtype=jnp.int32), :]
    att_rows = ordered[:, :, :head_dim].reshape(share_rows, total_width)
    gate_rows = ordered[:, :, head_dim:qu_cols].reshape(share_rows, total_width)
    x_rows = ordered[:, :, qu_cols:].reshape(share_rows, model_width)
    mean_value = jnp.mean(att_rows, axis=1, keepdims=True)
    variance = jnp.mean(att_rows * att_rows, axis=1, keepdims=True) - mean_value * mean_value
    hidden = (
        (att_rows - mean_value) * lax.rsqrt(variance + norm_eps) * norm_gain[None, :] * gate_rows
    ).astype(jnp.bfloat16)
    my_rows = x_rows + jnp.dot(hidden, w_out, preferred_element_type=jnp.float32)
    return my_rows.astype(jnp.bfloat16)


def silu(x):
    half = x * 0.5
    return half + half * jnp.tanh(half)


def item_kernel(
    devices,
    slots_ref,
    ranker_ref,
    blocks_ref,
    cand_ref,
    gain_ref,
    pool_ref,
    kv_ref,
    wqu_hbm,
    wout_hbm,
    out_ref,
    items,
    picked,
    history,
    wqu,
    wout,
    head_qu,
    partial,
    core_in,
    chip_sum,
    chip_in,
    hidden,
    table,
    onehot,
    load_sem,
    pool_send,
    pool_recv,
    kv_send,
    kv_recv,
    core_send,
    core_recv,
    chip_send,
    chip_recv,
    hid_send,
    hid_recv,
):
    me = lax.axis_index("rank")
    slots_here, head_count, block_len, pair_width = kv_ref.shape
    head_dim = pair_width // 2
    user_count, most_blocks = slots_ref.shape
    rows_here, model_width = pool_ref.shape
    item_count = devices * rows_here
    half_items = item_count // 2
    share_rows = out_ref.shape[0]
    team = devices // user_count
    bits = devices.bit_length() - 1
    score_scale = 1.0 / math.sqrt(head_dim)

    def bit_of(j):
        return (me // (1 << j)) % 2

    def flipped(mask):
        other = me
        for j in range(bits):
            if mask >> j & 1:
                other = other + (1 << j) * (1 - 2 * bit_of(j))
        return other

    my_group = me // team
    share = me % team
    core = bit_of(0)

    load_qu = pltpu.make_async_copy(wqu_hbm, wqu, load_sem.at[0])
    load_out = pltpu.make_async_copy(wout_hbm, wout, load_sem.at[1])
    load_qu.start()
    load_out.start()

    barrier = pltpu.get_barrier_semaphore()
    masks = [1, 2] + [team * d for d in range(1, user_count)]
    for mask in masks:
        pl.semaphore_signal(
            barrier, inc=1, device_id={"rank": flipped(mask)}, device_id_type=MESH
        )

    place = 0
    for j in range(bits):
        place = place + bit_of(j) * (1 << (bits - 1 - j))
    items[place] = pool_ref[...]
    held, alive = [], []
    for u in range(user_count):
        slot, live = jnp.int32(0), jnp.int32(0)
        for b in range(most_blocks):
            entry = slots_ref[u, b]
            mine = lax.div(entry, slots_here) == me
            slot = jnp.where(mine, lax.rem(entry, slots_here), slot)
            live = jnp.where(mine & (b < blocks_ref[u]), 1, live)
        held.append(slot)
        alive.append(live)
    for g in range(user_count):
        slot, live = jnp.int32(0), jnp.int32(0)
        for u in range(user_count):
            here = ranker_ref[u] == g
            slot = jnp.where(here, held[u], slot)
            live = jnp.where(here, alive[u], live)
        block = kv_ref[slot]
        picked[g] = jnp.where(live == 1, block, jnp.zeros_like(block))

    pl.semaphore_wait(barrier, len(masks))

    def pool_step(j):
        span = 1 << (bits - 1 - j)
        part = items.at[pl.ds((place // span) * span, span)]
        return pltpu.make_async_remote_copy(
            src_ref=part,
            dst_ref=part,
            send_sem=pool_send.at[j],
            recv_sem=pool_recv.at[j],
            device_id={"rank": flipped(1 << j)},
            device_id_type=MESH,
        )

    def kv_copy(h, d):
        other = flipped(team * d)
        return pltpu.make_async_remote_copy(
            src_ref=picked.at[other // team, h],
            dst_ref=history.at[h, d],
            send_sem=kv_send.at[h, d - 1],
            recv_sem=kv_recv.at[h, d - 1],
            device_id={"rank": other},
            device_id_type=MESH,
        )

    pool_step(bits - 1).start()
    kv_copies = {}
    for h in range(head_count):
        for d in reversed(range(1, user_count)):
            kv_copies[h, d] = kv_copy(h, d)
            kv_copies[h, d].start()

    for h in range(head_count):
        history[h, 0] = picked[my_group, h]

    first = pl.multiple_of(share * share_rows, share_rows)
    ids = jnp.zeros((1, share_rows), jnp.int32)
    for u in range(user_count):
        ids = jnp.where(ranker_ref[u] == my_group, cand_ref[pl.ds(u, 1), pl.ds(first, share_rows)], ids)
    row = lax.broadcasted_iota(jnp.int32, (item_count, share_rows), 0)
    block_at = row // rows_here
    rank_at = jnp.zeros_like(row)
    for j in range(bits):
        rank_at = rank_at + ((block_at >> j) & 1) * (1 << (bits - 1 - j))
    item_at = rank_at * rows_here + row % rows_here
    hits = (item_at == ids).astype(jnp.float32)
    onehot[...] = hits.T.astype(jnp.bfloat16)

    for j in reversed(range(bits)):
        step = pool_step(j)
        if j < bits - 1:
            step.start()
        step.wait()

    load_qu.wait()
    all_items = items[...].reshape(item_count, model_width)
    for h in range(head_count):
        qu = jnp.dot(
            all_items,
            wqu[:, h * pair_width : (h + 1) * pair_width],
            preferred_element_type=jnp.float32,
        )
        head_qu[h] = silu(qu).astype(jnp.bfloat16)

    mine_at = pl.multiple_of(core * half_items, half_items)
    other_at = pl.multiple_of((1 - core) * half_items, half_items)

    def core_copy(h):
        return pltpu.make_async_remote_copy(
            src_ref=partial.at[h, pl.ds(other_at, half_items)],
            dst_ref=core_in.at[h],
            send_sem=core_send.at[h],
            recv_sem=core_recv.at[h],
            device_id={"rank": flipped(1)},
            device_id_type=MESH,
        )

    def chip_copy(h):
        return pltpu.make_async_remote_copy(
            src_ref=chip_sum.at[h],
            dst_ref=chip_in.at[h],
            send_sem=chip_send.at[h],
            recv_sem=chip_recv.at[h],
            device_id={"rank": flipped(2)},
            device_id_type=MESH,
        )

    def to_chip(h):
        core_copy(h).wait()
        chip_sum[h] = partial[h, pl.ds(mine_at, half_items)] + core_in[h]
        chip_copy(h).start()

    for h in range(head_count):
        for d in range(1, user_count):
            kv_copies[h, d].wait()
        pairs = history[h].reshape(user_count * block_len, pair_width)
        scores = lax.dot_general(
            head_qu[h, :, :head_dim],
            pairs[:, :head_dim],
            (((1,), (1,)), ((), ())),
            preferred_element_type=jnp.float32,
        )
        weights = silu(scores * score_scale).astype(jnp.bfloat16)
        partial[h] = jnp.dot(weights, pairs[:, head_dim:], preferred_element_type=jnp.float32)
        core_copy(h).start()
        if h > 0:
            to_chip(h - 1)
    to_chip(head_count - 1)

    attended = []
    for h in range(head_count):
        chip_copy(h).wait()
        attended.append(chip_sum[h] + chip_in[h])
    width = head_count * head_dim
    mean = sum(jnp.sum(a, axis=1, keepdims=True) for a in attended) / width
    square = sum(jnp.sum(a * a, axis=1, keepdims=True) for a in attended) / width
    scale = lax.rsqrt(square - mean * mean + norm_eps)
    for h in range(head_count):
        columns = slice(h * head_dim, (h + 1) * head_dim)
        gate = head_qu[h, pl.ds(mine_at, half_items), head_dim:].astype(jnp.float32)
        normed = (attended[h] - mean) * scale * gain_ref[:, columns] * gate
        hidden[pl.ds(mine_at, half_items), columns] = normed.astype(jnp.bfloat16)

    own_half = hidden.at[pl.ds(mine_at, half_items)]
    swap = pltpu.make_async_remote_copy(
        src_ref=own_half,
        dst_ref=own_half,
        send_sem=hid_send,
        recv_sem=hid_recv,
        device_id={"rank": flipped(1)},
        device_id_type=MESH,
    )
    swap.start()
    load_out.wait()

    half_blocks = devices // 2

    def project(at, block_from):
        base = items[pl.ds(block_from, half_blocks)].reshape(half_items, model_width)
        mixed = base.astype(jnp.float32) + jnp.dot(
            hidden[pl.ds(at, half_items)], wout[...], preferred_element_type=jnp.float32
        )
        table[pl.ds(at, half_items)] = mixed.astype(jnp.bfloat16)

    project(mine_at, core * half_blocks)
    swap.wait()
    project(other_at, (1 - core) * half_blocks)
    out_ref[...] = jnp.dot(
        onehot[...], table[...], preferred_element_type=jnp.float32
    ).astype(jnp.bfloat16)


def item_body(pool, kv_cache, w_qu, w_out, norm_gain, cand_ids, ranker, hist_blocks, cache_slot):
    devices = lax.axis_size("rank")
    slots_here, head_count, block_len, pair_width = kv_cache.shape
    head_dim = pair_width // 2
    user_count = cache_slot.shape[0]
    rows_here, model_width = pool.shape
    item_count = devices * rows_here
    half_items = item_count // 2
    share_rows = cand_ids.shape[1] * user_count // devices
    width = head_count * head_dim
    bits = devices.bit_length() - 1
    smem = pl.BlockSpec(memory_space=pltpu.SMEM)
    vmem = pl.BlockSpec(memory_space=pltpu.VMEM)
    hbm = pl.BlockSpec(memory_space=pl.ANY)
    dma = pltpu.SemaphoreType.DMA
    narrow, wide = jnp.bfloat16, jnp.float32
    return pl.pallas_call(
        functools.partial(item_kernel, devices),
        out_shape=jax.ShapeDtypeStruct((share_rows, model_width), narrow),
        in_specs=[smem, smem, smem, vmem, vmem, vmem, vmem, hbm, hbm],
        out_specs=vmem,
        scratch_shapes=[
            pltpu.VMEM((devices, rows_here, model_width), narrow),
            pltpu.VMEM((user_count, head_count, block_len, pair_width), narrow),
            pltpu.VMEM((head_count, user_count, block_len, pair_width), narrow),
            pltpu.VMEM(w_qu.shape, narrow),
            pltpu.VMEM(w_out.shape, narrow),
            pltpu.VMEM((head_count, item_count, pair_width), narrow),
            pltpu.VMEM((head_count, item_count, head_dim), wide),
            pltpu.VMEM((head_count, half_items, head_dim), wide),
            pltpu.VMEM((head_count, half_items, head_dim), wide),
            pltpu.VMEM((head_count, half_items, head_dim), wide),
            pltpu.VMEM((item_count, width), narrow),
            pltpu.VMEM((item_count, model_width), narrow),
            pltpu.VMEM((share_rows, item_count), narrow),
            dma((2,)),
            dma((bits,)),
            dma((bits,)),
            dma((head_count, user_count - 1)),
            dma((head_count, user_count - 1)),
            dma((head_count,)),
            dma((head_count,)),
            dma((head_count,)),
            dma((head_count,)),
            dma,
            dma,
        ],
        compiler_params=pltpu.CompilerParams(
            collective_id=0, has_side_effects=True, vmem_limit_bytes=40 * 1024 * 1024
        ),
    )(
        cache_slot,
        ranker,
        hist_blocks,
        cand_ids,
        norm_gain.reshape(1, width),
        pool,
        kv_cache,
        w_qu,
        w_out,
    )


def body(pool, kv_cache, w_qu, w_out, norm_gain, cand_ids, ranker, hist_blocks, cache_slot):
    devices = lax.axis_size("rank")
    user_count = cache_slot.shape[0]
    items_fit = pool.shape[0] * devices * devices <= cand_ids.shape[1] * user_count
    in_fours = devices == 4 * user_count and devices & (devices - 1) == 0
    chosen = item_body if items_fit and in_fours and pool.shape[0] % 16 == 0 else candidate_body
    return chosen(
        pool, kv_cache, w_qu, w_out, norm_gain, cand_ids, ranker, hist_blocks, cache_slot
    )


def solution(mesh):
    in_specs = (
        P(("groups", "rank"), None),
        P(("groups", "rank"), None, None, None),
        P(),
        P(),
        P(),
        P("groups", None),
        P(),
        P("groups"),
        P("groups", None),
    )
    out_specs = P(("groups", "rank"), None)
    return jax.shard_map(body, mesh=mesh, in_specs=in_specs, out_specs=out_specs, check_vma=False)
```

```python
import functools
import math

import jax
import jax.numpy as jnp
from jax import lax
from jax.experimental import pallas as pl
from jax.experimental.pallas import tpu as pltpu
from jax.sharding import PartitionSpec as P

norm_eps = 1e-05
MESH = pl.DeviceIdType.MESH


def partner(shard, axis, bit):
    return lax.ppermute(shard, axis, [(i, i ^ 1 << bit) for i in range(lax.axis_size(axis))])


def attend_blocks(queries, stacked, head_dim, live_steps):
    score_scale = 1.0 / math.sqrt(head_dim)

    def step_fn(running, item):
        step_index, key_block = item

        def compute(total):
            key_part = key_block[:, :head_dim]
            value_part = key_block[:, head_dim:]
            scores = lax.dot_general(
                queries, key_part, (((1,), (1,)), ((), ())), preferred_element_type=jnp.float32
            )
            weights = jax.nn.silu(scores * score_scale).astype(jnp.bfloat16)
            return total + jnp.dot(weights, value_part, preferred_element_type=jnp.float32)

        def keep_same(total):
            return total

        return (lax.cond(step_index < live_steps, compute, keep_same, running), None)

    initial = jnp.zeros((queries.shape[0], head_dim), jnp.float32)
    step_ids = jnp.arange(stacked.shape[0], dtype=jnp.int32)
    attended, unused = lax.scan(step_fn, initial, (step_ids, stacked))
    return attended


def candidate_body(pool, kv_cache, w_qu, w_out, norm_gain, cand_ids, ranker, hist_blocks, cache_slot):
    devices = lax.axis_size("rank")
    my_index = lax.axis_index("rank")
    slots_here, head_count, block_len, pair_width = kv_cache.shape
    head_dim = pair_width // 2
    user_count, most_blocks = cache_slot.shape
    model_width = pool.shape[1]
    cand_count = cand_ids.shape[1]
    slice_width = model_width // head_count
    qu_cols = 2 * head_dim
    my_group = my_index // head_count
    my_head = my_index % head_count
    bit_count = head_count.bit_length() - 1
    share_rows = cand_count // head_count
    user_range = jnp.arange(user_count, dtype=jnp.int32)
    group_match = ranker[None, :] == user_range[:, None]
    user_of_group = jnp.sum(jnp.where(group_match, user_range[None, :], 0), axis=1)
    my_user = jnp.sum(jnp.where(user_range == my_group, user_of_group, 0))
    block_range = jnp.arange(most_blocks, dtype=jnp.int32)
    live_blocks = block_range[None, :] < hist_blocks[:, None]
    owner_table = cache_slot // slots_here
    held_here = live_blocks & (owner_table == my_index)
    held_slot = jnp.sum(jnp.where(held_here, cache_slot % slots_here, 0), axis=1)
    held_flag = jnp.any(held_here, axis=1)
    slot_of_group = jnp.sum(jnp.where(group_match, held_slot[None, :], 0), axis=1)
    flag_of_group = jnp.any(group_match & held_flag[None, :], axis=1)
    outgoing = jnp.take(kv_cache, slot_of_group, axis=0)
    outgoing = jnp.where(flag_of_group[:, None, None, None], outgoing, jnp.zeros_like(outgoing))
    outgoing = outgoing.reshape(devices, block_len, pair_width)
    incoming = lax.all_to_all(outgoing, "rank", split_axis=0, concat_axis=0, tiled=True)
    my_ids = lax.dynamic_index_in_dim(cand_ids, my_user, 0, keepdims=False)
    whole_pool = lax.all_gather(pool, "rank", axis=0, tiled=True)
    cand_rows = jnp.take(whole_pool, my_ids, axis=0)
    w_head = lax.dynamic_slice_in_dim(w_qu, my_head * qu_cols, qu_cols, 1)
    head_qu = jax.nn.silu(jnp.dot(cand_rows, w_head, preferred_element_type=jnp.float32)).astype(
        jnp.bfloat16
    )
    x_part = lax.dynamic_slice_in_dim(cand_rows, my_head * slice_width, slice_width, 1)
    queries = head_qu[:, :head_dim]
    gate_part = head_qu[:, head_dim:]
    step_sources = min(16, devices)
    stacked = incoming.reshape(devices // step_sources, step_sources * block_len, pair_width)
    live_steps = stacked.shape[0]
    attended = attend_blocks(queries, stacked, head_dim, live_steps)
    total_width = head_count * head_dim
    carried = jnp.concatenate(
        [attended, gate_part.astype(jnp.float32), x_part.astype(jnp.float32)], axis=1
    )
    state = carried.reshape(head_count, share_rows, 1, carried.shape[1])
    for bit_index in reversed(range(bit_count)):
        half_count = state.shape[0] // 2
        lower_half = state[:half_count]
        upper_half = state[half_count:]
        upper_side = my_head >> bit_index & 1 == 1
        keeping = jnp.where(upper_side, upper_half, lower_half)
        giving = jnp.where(upper_side, lower_half, upper_half)
        received = partner(giving, "rank", bit_index)
        state = jnp.where(
            upper_side,
            jnp.concatenate([received, keeping], axis=2),
            jnp.concatenate([keeping, received], axis=2),
        )
    reversal = [
        sum(((source >> bit & 1) << bit_count - 1 - bit for bit in range(bit_count)))
        for source in range(head_count)
    ]
    ordered = state[0][:, jnp.array(reversal, dtype=jnp.int32), :]
    att_rows = ordered[:, :, :head_dim].reshape(share_rows, total_width)
    gate_rows = ordered[:, :, head_dim:qu_cols].reshape(share_rows, total_width)
    x_rows = ordered[:, :, qu_cols:].reshape(share_rows, model_width)
    mean_value = jnp.mean(att_rows, axis=1, keepdims=True)
    variance = jnp.mean(att_rows * att_rows, axis=1, keepdims=True) - mean_value * mean_value
    hidden = (
        (att_rows - mean_value) * lax.rsqrt(variance + norm_eps) * norm_gain[None, :] * gate_rows
    ).astype(jnp.bfloat16)
    my_rows = x_rows + jnp.dot(hidden, w_out, preferred_element_type=jnp.float32)
    return my_rows.astype(jnp.bfloat16)


def silu(x):
    half = x * 0.5
    return half + half * jnp.tanh(half)


def item_kernel(
    devices,
    slots_hbm,
    ranker_hbm,
    blocks_hbm,
    cand_hbm,
    gain_hbm,
    pool_hbm,
    kv_hbm,
    wqu_hbm,
    wout_hbm,
    out_ref,
    slots_ref,
    ranker_ref,
    blocks_ref,
    cand_ref,
    gain_ref,
    kv_ref,
    items,
    picked,
    history,
    wqu,
    wout,
    head_qu,
    partial,
    core_in,
    chip_sum,
    chip_in,
    hidden,
    table,
    onehot,
    load_sem,
    pool_send,
    pool_recv,
    kv_send,
    kv_recv,
    core_send,
    core_recv,
    chip_send,
    chip_recv,
    hid_send,
    hid_recv,
):
    me = lax.axis_index("rank")
    slots_here, head_count, block_len, pair_width = kv_ref.shape
    head_dim = pair_width // 2
    user_count, most_blocks = slots_ref.shape
    rows_here, model_width = pool_hbm.shape
    item_count = devices * rows_here
    half_items = item_count // 2
    share_rows = out_ref.shape[0]
    team = devices // user_count
    bits = devices.bit_length() - 1
    score_scale = 1.0 / math.sqrt(head_dim)

    def bit_of(j):
        return (me // (1 << j)) % 2

    def flipped(mask):
        other = me
        for j in range(bits):
            if mask >> j & 1:
                other = other + (1 << j) * (1 - 2 * bit_of(j))
        return other

    my_group = me // team
    share = me % team
    core = bit_of(0)

    place = 0
    for j in range(bits):
        place = place + bit_of(j) * (1 << (bits - 1 - j))

    loads = [
        pltpu.make_async_copy(source, target, load_sem.at[i])
        for i, (source, target) in enumerate(
            (
                (slots_hbm, slots_ref),
                (ranker_hbm, ranker_ref),
                (blocks_hbm, blocks_ref),
                (pool_hbm, items.at[place]),
                (kv_hbm, kv_ref),
                (cand_hbm, cand_ref),
                (gain_hbm, gain_ref),
                (wqu_hbm, wqu),
                (wout_hbm, wout),
            )
        )
    ]
    for load in loads:
        load.start()
    load_slots, load_ranker, load_blocks, load_pool, load_kv = loads[:5]
    load_cand, load_gain, load_qu, load_out = loads[5:]

    barrier = pltpu.get_barrier_semaphore()
    masks = [1, 2] + [team * d for d in range(1, user_count)]
    for mask in masks:
        pl.semaphore_signal(
            barrier, inc=1, device_id={"rank": flipped(mask)}, device_id_type=MESH
        )

    load_slots.wait()
    load_ranker.wait()
    load_blocks.wait()
    held, alive = [], []
    for u in range(user_count):
        slot, live = jnp.int32(0), jnp.int32(0)
        for b in range(most_blocks):
            entry = slots_ref[u, b]
            mine = lax.div(entry, slots_here) == me
            slot = jnp.where(mine, lax.rem(entry, slots_here), slot)
            live = jnp.where(mine & (b < blocks_ref[u]), 1, live)
        held.append(slot)
        alive.append(live)
    pl.semaphore_wait(barrier, len(masks))

    def pool_step(j):
        span = 1 << (bits - 1 - j)
        part = items.at[pl.ds((place // span) * span, span)]
        return pltpu.make_async_remote_copy(
            src_ref=part,
            dst_ref=part,
            send_sem=pool_send.at[j],
            recv_sem=pool_recv.at[j],
            device_id={"rank": flipped(1 << j)},
            device_id_type=MESH,
        )

    def kv_copy(h, d):
        return pltpu.make_async_remote_copy(
            src_ref=picked.at[d - 1, h],
            dst_ref=history.at[h, d],
            send_sem=kv_send.at[h, d - 1],
            recv_sem=kv_recv.at[h, d - 1],
            device_id={"rank": flipped(team * d)},
            device_id_type=MESH,
        )

    far_first = range(user_count - 1, 0, -1)

    def send_head(h):
        for d in far_first:
            kv_copy(h, d).start()

    load_pool.wait()
    pool_step(bits - 1).start()

    load_kv.wait()
    for d in (*far_first, 0):
        group = flipped(team * d) // team
        slot, live = jnp.int32(0), jnp.int32(0)
        for u in range(user_count):
            here = ranker_ref[u] == group
            slot = jnp.where(here, held[u], slot)
            live = jnp.where(here, alive[u], live)
        block = kv_ref[slot]
        block = jnp.where(live == 1, block, jnp.zeros_like(block))
        if d > 0:
            picked[d - 1] = block
            kv_copy(0, d).start()
        else:
            history[:, 0] = block

    waves = list(range(1, head_count))
    for j in range(bits - 1, 1, -1):
        pool_step(j).wait()
        pool_step(j - 1).start()
        if waves:
            send_head(waves.pop(0))

    load_cand.wait()
    first = pl.multiple_of(share * share_rows, share_rows)
    ids = jnp.zeros((1, share_rows), jnp.int32)
    for u in range(user_count):
        ids = jnp.where(ranker_ref[u] == my_group, cand_ref[pl.ds(u, 1), pl.ds(first, share_rows)], ids)
    row = lax.broadcasted_iota(jnp.int32, (item_count, share_rows), 0)
    block_at = row // rows_here
    rank_at = jnp.zeros_like(row)
    for j in range(bits):
        rank_at = rank_at + ((block_at >> j) & 1) * (1 << (bits - 1 - j))
    item_at = rank_at * rows_here + row % rows_here
    hits = (item_at == ids).astype(jnp.float32)
    onehot[...] = hits.T.astype(jnp.bfloat16)

    half_blocks = devices // 2
    load_qu.wait()

    def project_in(at, block_from):
        some = items[pl.ds(block_from, half_blocks)].reshape(half_items, model_width)
        for h in range(head_count):
            qu = jnp.dot(
                some,
                wqu[:, h * pair_width : (h + 1) * pair_width],
                preferred_element_type=jnp.float32,
            )
            head_qu[h, pl.ds(at, half_items)] = silu(qu).astype(jnp.bfloat16)

    mine_at = pl.multiple_of(core * half_items, half_items)
    other_at = pl.multiple_of((1 - core) * half_items, half_items)

    pool_step(1).wait()
    pool_step(0).start()
    for h in waves:
        send_head(h)
    project_in(mine_at, core * half_blocks)
    pool_step(0).wait()
    project_in(other_at, (1 - core) * half_blocks)

    def core_copy(h):
        return pltpu.make_async_remote_copy(
            src_ref=partial.at[h, pl.ds(other_at, half_items)],
            dst_ref=core_in.at[h],
            send_sem=core_send.at[h],
            recv_sem=core_recv.at[h],
            device_id={"rank": flipped(1)},
            device_id_type=MESH,
        )

    def chip_copy(h):
        return pltpu.make_async_remote_copy(
            src_ref=chip_sum.at[h],
            dst_ref=chip_in.at[h],
            send_sem=chip_send.at[h],
            recv_sem=chip_recv.at[h],
            device_id={"rank": flipped(2)},
            device_id_type=MESH,
        )

    def to_chip(h):
        core_copy(h).wait()
        chip_sum[h] = partial[h, pl.ds(mine_at, half_items)] + core_in[h]
        chip_copy(h).start()

    for h in range(head_count):
        for d in range(1, user_count):
            kv_copy(h, d).wait()
        pairs = history[h].reshape(user_count * block_len, pair_width)
        scores = lax.dot_general(
            head_qu[h, :, :head_dim],
            pairs[:, :head_dim],
            (((1,), (1,)), ((), ())),
            preferred_element_type=jnp.float32,
        )
        weights = silu(scores * score_scale).astype(jnp.bfloat16)
        partial[h] = jnp.dot(weights, pairs[:, head_dim:], preferred_element_type=jnp.float32)
        core_copy(h).start()
        if h > 0:
            to_chip(h - 1)
    to_chip(head_count - 1)

    attended = []
    for h in range(head_count):
        chip_copy(h).wait()
        attended.append(chip_sum[h] + chip_in[h])
    width = head_count * head_dim
    mean = sum(jnp.sum(a, axis=1, keepdims=True) for a in attended) / width
    square = sum(jnp.sum(a * a, axis=1, keepdims=True) for a in attended) / width
    scale = lax.rsqrt(square - mean * mean + norm_eps)
    load_gain.wait()
    for h in range(head_count):
        columns = slice(h * head_dim, (h + 1) * head_dim)
        gate = head_qu[h, pl.ds(mine_at, half_items), head_dim:].astype(jnp.float32)
        normed = (attended[h] - mean) * scale * gain_ref[:, columns] * gate
        hidden[pl.ds(mine_at, half_items), columns] = normed.astype(jnp.bfloat16)

    own_half = hidden.at[pl.ds(mine_at, half_items)]
    swap = pltpu.make_async_remote_copy(
        src_ref=own_half,
        dst_ref=own_half,
        send_sem=hid_send,
        recv_sem=hid_recv,
        device_id={"rank": flipped(1)},
        device_id_type=MESH,
    )
    swap.start()
    load_out.wait()

    def project(at, block_from):
        base = items[pl.ds(block_from, half_blocks)].reshape(half_items, model_width)
        mixed = base.astype(jnp.float32) + jnp.dot(
            hidden[pl.ds(at, half_items)], wout[...], preferred_element_type=jnp.float32
        )
        table[pl.ds(at, half_items)] = mixed.astype(jnp.bfloat16)

    project(mine_at, core * half_blocks)
    swap.wait()
    project(other_at, (1 - core) * half_blocks)
    out_ref[...] = jnp.dot(
        onehot[...], table[...], preferred_element_type=jnp.float32
    ).astype(jnp.bfloat16)


def item_body(pool, kv_cache, w_qu, w_out, norm_gain, cand_ids, ranker, hist_blocks, cache_slot):
    devices = lax.axis_size("rank")
    slots_here, head_count, block_len, pair_width = kv_cache.shape
    head_dim = pair_width // 2
    user_count = cache_slot.shape[0]
    rows_here, model_width = pool.shape
    item_count = devices * rows_here
    half_items = item_count // 2
    share_rows = cand_ids.shape[1] * user_count // devices
    width = head_count * head_dim
    bits = devices.bit_length() - 1
    vmem = pl.BlockSpec(memory_space=pltpu.VMEM)
    hbm = pl.BlockSpec(memory_space=pltpu.HBM)
    dma = pltpu.SemaphoreType.DMA
    narrow, wide = jnp.bfloat16, jnp.float32
    return pl.pallas_call(
        functools.partial(item_kernel, devices),
        out_shape=jax.ShapeDtypeStruct((share_rows, model_width), narrow),
        in_specs=[hbm] * 9,
        out_specs=vmem,
        scratch_shapes=[
            pltpu.SMEM(cache_slot.shape, jnp.int32),
            pltpu.SMEM(ranker.shape, jnp.int32),
            pltpu.SMEM(hist_blocks.shape, jnp.int32),
            pltpu.VMEM(cand_ids.shape, jnp.int32),
            pltpu.VMEM((1, width), wide),
            pltpu.VMEM(kv_cache.shape, narrow),
            pltpu.VMEM((devices, rows_here, model_width), narrow),
            pltpu.VMEM((user_count - 1, head_count, block_len, pair_width), narrow),
            pltpu.VMEM((head_count, user_count, block_len, pair_width), narrow),
            pltpu.VMEM(w_qu.shape, narrow),
            pltpu.VMEM(w_out.shape, narrow),
            pltpu.VMEM((head_count, item_count, pair_width), narrow),
            pltpu.VMEM((head_count, item_count, head_dim), wide),
            pltpu.VMEM((head_count, half_items, head_dim), wide),
            pltpu.VMEM((head_count, half_items, head_dim), wide),
            pltpu.VMEM((head_count, half_items, head_dim), wide),
            pltpu.VMEM((item_count, width), narrow),
            pltpu.VMEM((item_count, model_width), narrow),
            pltpu.VMEM((share_rows, item_count), narrow),
            dma((9,)),
            dma((bits,)),
            dma((bits,)),
            dma((head_count, user_count - 1)),
            dma((head_count, user_count - 1)),
            dma((head_count,)),
            dma((head_count,)),
            dma((head_count,)),
            dma((head_count,)),
            dma,
            dma,
        ],
        compiler_params=pltpu.CompilerParams(
            collective_id=0, has_side_effects=True, vmem_limit_bytes=62 * 1024 * 1024
        ),
    )(
        cache_slot,
        ranker,
        hist_blocks,
        cand_ids,
        norm_gain.reshape(1, width),
        pool,
        kv_cache,
        w_qu,
        w_out,
    )


def body(pool, kv_cache, w_qu, w_out, norm_gain, cand_ids, ranker, hist_blocks, cache_slot):
    devices = lax.axis_size("rank")
    user_count = cache_slot.shape[0]
    items_fit = pool.shape[0] * devices * devices <= cand_ids.shape[1] * user_count
    in_fours = devices == 4 * user_count and devices & (devices - 1) == 0
    chosen = item_body if items_fit and in_fours and pool.shape[0] % 16 == 0 else candidate_body
    return chosen(
        pool, kv_cache, w_qu, w_out, norm_gain, cand_ids, ranker, hist_blocks, cache_slot
    )


def solution(mesh):
    in_specs = (
        P(("groups", "rank"), None),
        P(("groups", "rank"), None, None, None),
        P(),
        P(),
        P(),
        P("groups", None),
        P(),
        P("groups"),
        P("groups", None),
    )
    out_specs = P(("groups", "rank"), None)
    return jax.shard_map(body, mesh=mesh, in_specs=in_specs, out_specs=out_specs, check_vma=False)
```

```python
import functools
import math

import jax
import jax.numpy as jnp
from jax import lax
from jax.experimental import pallas as pl
from jax.experimental.pallas import tpu as pltpu
from jax.sharding import PartitionSpec as P

norm_eps = 1e-05
MESH = pl.DeviceIdType.MESH


def partner(shard, axis, bit):
    return lax.ppermute(shard, axis, [(i, i ^ 1 << bit) for i in range(lax.axis_size(axis))])


def attend_blocks(queries, stacked, head_dim, live_steps):
    score_scale = 1.0 / math.sqrt(head_dim)

    def step_fn(running, item):
        step_index, key_block = item

        def compute(total):
            key_part = key_block[:, :head_dim]
            value_part = key_block[:, head_dim:]
            scores = lax.dot_general(
                queries, key_part, (((1,), (1,)), ((), ())), preferred_element_type=jnp.float32
            )
            weights = jax.nn.silu(scores * score_scale).astype(jnp.bfloat16)
            return total + jnp.dot(weights, value_part, preferred_element_type=jnp.float32)

        def keep_same(total):
            return total

        return (lax.cond(step_index < live_steps, compute, keep_same, running), None)

    initial = jnp.zeros((queries.shape[0], head_dim), jnp.float32)
    step_ids = jnp.arange(stacked.shape[0], dtype=jnp.int32)
    attended, unused = lax.scan(step_fn, initial, (step_ids, stacked))
    return attended


def candidate_body(pool, kv_cache, w_qu, w_out, norm_gain, cand_ids, ranker, hist_blocks, cache_slot):
    devices = lax.axis_size("rank")
    my_index = lax.axis_index("rank")
    slots_here, head_count, block_len, pair_width = kv_cache.shape
    head_dim = pair_width // 2
    user_count, most_blocks = cache_slot.shape
    model_width = pool.shape[1]
    cand_count = cand_ids.shape[1]
    slice_width = model_width // head_count
    qu_cols = 2 * head_dim
    my_group = my_index // head_count
    my_head = my_index % head_count
    bit_count = head_count.bit_length() - 1
    share_rows = cand_count // head_count
    user_range = jnp.arange(user_count, dtype=jnp.int32)
    group_match = ranker[None, :] == user_range[:, None]
    user_of_group = jnp.sum(jnp.where(group_match, user_range[None, :], 0), axis=1)
    my_user = jnp.sum(jnp.where(user_range == my_group, user_of_group, 0))
    block_range = jnp.arange(most_blocks, dtype=jnp.int32)
    live_blocks = block_range[None, :] < hist_blocks[:, None]
    owner_table = cache_slot // slots_here
    held_here = live_blocks & (owner_table == my_index)
    held_slot = jnp.sum(jnp.where(held_here, cache_slot % slots_here, 0), axis=1)
    held_flag = jnp.any(held_here, axis=1)
    slot_of_group = jnp.sum(jnp.where(group_match, held_slot[None, :], 0), axis=1)
    flag_of_group = jnp.any(group_match & held_flag[None, :], axis=1)
    outgoing = jnp.take(kv_cache, slot_of_group, axis=0)
    outgoing = jnp.where(flag_of_group[:, None, None, None], outgoing, jnp.zeros_like(outgoing))
    outgoing = outgoing.reshape(devices, block_len, pair_width)
    incoming = lax.all_to_all(outgoing, "rank", split_axis=0, concat_axis=0, tiled=True)
    my_ids = lax.dynamic_index_in_dim(cand_ids, my_user, 0, keepdims=False)
    whole_pool = lax.all_gather(pool, "rank", axis=0, tiled=True)
    cand_rows = jnp.take(whole_pool, my_ids, axis=0)
    w_head = lax.dynamic_slice_in_dim(w_qu, my_head * qu_cols, qu_cols, 1)
    head_qu = jax.nn.silu(jnp.dot(cand_rows, w_head, preferred_element_type=jnp.float32)).astype(
        jnp.bfloat16
    )
    x_part = lax.dynamic_slice_in_dim(cand_rows, my_head * slice_width, slice_width, 1)
    queries = head_qu[:, :head_dim]
    gate_part = head_qu[:, head_dim:]
    step_sources = min(16, devices)
    stacked = incoming.reshape(devices // step_sources, step_sources * block_len, pair_width)
    live_steps = stacked.shape[0]
    attended = attend_blocks(queries, stacked, head_dim, live_steps)
    total_width = head_count * head_dim
    carried = jnp.concatenate(
        [attended, gate_part.astype(jnp.float32), x_part.astype(jnp.float32)], axis=1
    )
    state = carried.reshape(head_count, share_rows, 1, carried.shape[1])
    for bit_index in reversed(range(bit_count)):
        half_count = state.shape[0] // 2
        lower_half = state[:half_count]
        upper_half = state[half_count:]
        upper_side = my_head >> bit_index & 1 == 1
        keeping = jnp.where(upper_side, upper_half, lower_half)
        giving = jnp.where(upper_side, lower_half, upper_half)
        received = partner(giving, "rank", bit_index)
        state = jnp.where(
            upper_side,
            jnp.concatenate([received, keeping], axis=2),
            jnp.concatenate([keeping, received], axis=2),
        )
    reversal = [
        sum(((source >> bit & 1) << bit_count - 1 - bit for bit in range(bit_count)))
        for source in range(head_count)
    ]
    ordered = state[0][:, jnp.array(reversal, dtype=jnp.int32), :]
    att_rows = ordered[:, :, :head_dim].reshape(share_rows, total_width)
    gate_rows = ordered[:, :, head_dim:qu_cols].reshape(share_rows, total_width)
    x_rows = ordered[:, :, qu_cols:].reshape(share_rows, model_width)
    mean_value = jnp.mean(att_rows, axis=1, keepdims=True)
    variance = jnp.mean(att_rows * att_rows, axis=1, keepdims=True) - mean_value * mean_value
    hidden = (
        (att_rows - mean_value) * lax.rsqrt(variance + norm_eps) * norm_gain[None, :] * gate_rows
    ).astype(jnp.bfloat16)
    my_rows = x_rows + jnp.dot(hidden, w_out, preferred_element_type=jnp.float32)
    return my_rows.astype(jnp.bfloat16)


def silu(x):
    half = x * 0.5
    return half + half * jnp.tanh(half)


def item_kernel(
    devices,
    slots_hbm,
    ranker_hbm,
    blocks_hbm,
    cand_hbm,
    gain_hbm,
    pool_hbm,
    kv_hbm,
    wqu_hbm,
    wout_hbm,
    table_hbm,
    onehot_hbm,
    slots_ref,
    ranker_ref,
    blocks_ref,
    cand_ref,
    gain_ref,
    kv_ref,
    items,
    picked,
    history,
    wqu,
    wout,
    head_qu,
    partial,
    core_in,
    chip_sum,
    chip_out,
    chip_in,
    hidden,
    table,
    onehot,
    load_sem,
    store_sem,
    pool_send,
    pool_recv,
    kv_send,
    kv_recv,
    core_send,
    core_recv,
    chip_send,
    chip_recv,
    hid_send,
    hid_recv,
):
    me = lax.axis_index("rank")
    slots_here, head_count, block_len, pair_width = kv_ref.shape
    head_dim = pair_width // 2
    user_count, most_blocks = slots_ref.shape
    rows_here, model_width = pool_hbm.shape
    item_count = devices * rows_here
    half_items = item_count // 2
    share_rows = onehot_hbm.shape[0]
    team = devices // user_count
    bits = devices.bit_length() - 1
    score_scale = 1.0 / math.sqrt(head_dim)

    my_bits = [lax.rem(lax.div(me, 1 << j), 2) for j in range(bits)]

    def bit_of(j):
        return my_bits[j]

    def flipped(mask):
        other = me
        for j in range(bits):
            if mask >> j & 1:
                other = other + (1 << j) * (1 - 2 * bit_of(j))
        return other

    my_group = lax.div(me, team)
    share = lax.rem(me, team)
    core = bit_of(0)

    place = 0
    for j in range(bits):
        place = place + bit_of(j) * (1 << (bits - 1 - j))

    loads = [
        pltpu.make_async_copy(source, target, load_sem.at[i])
        for i, (source, target) in enumerate(
            (
                (slots_hbm, slots_ref),
                (ranker_hbm, ranker_ref),
                (blocks_hbm, blocks_ref),
                (pool_hbm, items.at[place]),
                (kv_hbm, kv_ref),
                (cand_hbm, cand_ref),
                (gain_hbm, gain_ref),
                (wqu_hbm, wqu),
                (wout_hbm, wout),
            )
        )
    ]
    for load in loads:
        load.start()
    load_slots, load_ranker, load_blocks, load_pool, load_kv = loads[:5]
    load_cand, load_gain, load_qu, load_out = loads[5:]

    barrier = pltpu.get_barrier_semaphore()
    masks = [1, 2] + [team * d for d in range(1, user_count)]
    for mask in masks:
        pl.semaphore_signal(
            barrier, inc=1, device_id={"rank": flipped(mask)}, device_id_type=MESH
        )

    load_slots.wait()
    load_ranker.wait()
    load_blocks.wait()
    first_slot = me * slots_here
    held, alive = [], []
    for u in range(user_count):
        slot, live = jnp.int32(0), jnp.int32(0)
        for b in range(most_blocks):
            entry = slots_ref[u, b]
            offset = entry - first_slot
            mine = (offset >= 0) & (offset < slots_here)
            slot = jnp.where(mine, offset, slot)
            live = jnp.where(mine & (b < blocks_ref[u]), 1, live)
        held.append(slot)
        alive.append(live)
    pl.semaphore_wait(barrier, len(masks))

    def pool_step(j):
        span = 1 << (bits - 1 - j)
        part = items.at[pl.ds(lax.div(place, span) * span, span)]
        return pltpu.make_async_remote_copy(
            src_ref=part,
            dst_ref=part,
            send_sem=pool_send.at[j],
            recv_sem=pool_recv.at[j],
            device_id={"rank": flipped(1 << j)},
            device_id_type=MESH,
        )

    def kv_copy(h, d):
        return pltpu.make_async_remote_copy(
            src_ref=picked.at[d - 1, h],
            dst_ref=history.at[h, d],
            send_sem=kv_send.at[h, d - 1],
            recv_sem=kv_recv.at[h, d - 1],
            device_id={"rank": flipped(team * d)},
            device_id_type=MESH,
        )

    far_first = range(user_count - 1, 0, -1)

    def send_head(h):
        for d in far_first:
            kv_copy(h, d).start()

    load_pool.wait()
    pool_step(bits - 1).start()

    load_kv.wait()
    for d in (*far_first, 0):
        group = lax.div(flipped(team * d), team)
        slot, live = jnp.int32(0), jnp.int32(0)
        for u in range(user_count):
            here = ranker_ref[u] == group
            slot = jnp.where(here, held[u], slot)
            live = jnp.where(here, alive[u], live)
        block = kv_ref[slot]
        block = jnp.where(live == 1, block, jnp.zeros_like(block))
        if d > 0:
            picked[d - 1] = block
            kv_copy(0, d).start()
        else:
            history[:, 0] = block

    waves = list(range(1, head_count))
    for j in range(bits - 1, 1, -1):
        pool_step(j).wait()
        pool_step(j - 1).start()
        if waves:
            send_head(waves.pop(0))

    load_cand.wait()
    first = pl.multiple_of(share * share_rows, share_rows)
    ids = jnp.zeros((1, share_rows), jnp.int32)
    for u in range(user_count):
        ids = jnp.where(ranker_ref[u] == my_group, cand_ref[pl.ds(u, 1), pl.ds(first, share_rows)], ids)
    row = lax.broadcasted_iota(jnp.int32, (rows_here, share_rows), 0)
    hits = []
    for at in range(devices):
        rank_at = sum((at >> j & 1) << bits - 1 - j for j in range(bits))
        hits.append((row + rank_at * rows_here == ids).astype(jnp.float32))
    onehot[...] = jnp.concatenate(hits, axis=0).T.astype(jnp.bfloat16)
    store_onehot = pltpu.make_async_copy(onehot, onehot_hbm, store_sem.at[0])
    store_onehot.start()

    half_blocks = devices // 2
    load_qu.wait()

    def project_in(at, block_from):
        some = items[pl.ds(block_from, half_blocks)].reshape(half_items, model_width)
        for h in range(head_count):
            qu = jnp.dot(
                some,
                wqu[:, h * pair_width : (h + 1) * pair_width],
                preferred_element_type=jnp.float32,
            )
            head_qu[h, pl.ds(at, half_items)] = silu(qu).astype(jnp.bfloat16)

    mine_at = pl.multiple_of(core * half_items, half_items)
    other_at = pl.multiple_of((1 - core) * half_items, half_items)

    pool_step(1).wait()
    pool_step(0).start()
    for h in waves:
        send_head(h)
    project_in(mine_at, core * half_blocks)
    pool_step(0).wait()
    project_in(other_at, (1 - core) * half_blocks)

    def core_copy(h):
        return pltpu.make_async_remote_copy(
            src_ref=partial.at[h, pl.ds(other_at, half_items)],
            dst_ref=core_in.at[h],
            send_sem=core_send.at[h],
            recv_sem=core_recv.at[h],
            device_id={"rank": flipped(1)},
            device_id_type=MESH,
        )

    def chip_copy(h):
        return pltpu.make_async_remote_copy(
            src_ref=chip_out.at[h],
            dst_ref=chip_in.at[h],
            send_sem=chip_send.at[h],
            recv_sem=chip_recv.at[h],
            device_id={"rank": flipped(2)},
            device_id_type=MESH,
        )

    def to_chip(h):
        core_copy(h).wait()
        chip_sum[h] = partial[h, pl.ds(mine_at, half_items)] + core_in[h]
        chip_out[h] = chip_sum[h].astype(jnp.bfloat16)
        chip_copy(h).start()

    for h in range(head_count):
        for d in range(1, user_count):
            kv_copy(h, d).wait()
        pairs = history[h].reshape(user_count * block_len, pair_width)
        for at in (other_at, mine_at):
            scores = lax.dot_general(
                head_qu[h, pl.ds(at, half_items), :head_dim],
                pairs[:, :head_dim],
                (((1,), (1,)), ((), ())),
                preferred_element_type=jnp.float32,
            )
            weights = silu(scores * score_scale).astype(jnp.bfloat16)
            partial[h, pl.ds(at, half_items)] = jnp.dot(
                weights, pairs[:, head_dim:], preferred_element_type=jnp.float32
            )
            if at is other_at:
                core_copy(h).start()
        if h > 0:
            to_chip(h - 1)
    to_chip(head_count - 1)

    load_gain.wait()
    load_out.wait()
    width = head_count * head_dim
    attended, mean, square = [], 0.0, 0.0
    for h in range(head_count):
        chip_copy(h).wait()
        one = chip_sum[h] + chip_in[h].astype(jnp.float32)
        mean = mean + jnp.sum(one, axis=1, keepdims=True)
        square = square + jnp.sum(one * one, axis=1, keepdims=True)
        attended.append(one)
    mean = mean / width
    square = square / width
    scale = lax.rsqrt(square - mean * mean + norm_eps)
    for h in range(head_count):
        columns = slice(h * head_dim, (h + 1) * head_dim)
        gate = head_qu[h, pl.ds(mine_at, half_items), head_dim:].astype(jnp.float32)
        normed = (attended[h] - mean) * scale * gain_ref[:, columns] * gate
        hidden[pl.ds(mine_at, half_items), columns] = normed.astype(jnp.bfloat16)

    own_half = hidden.at[pl.ds(mine_at, half_items)]
    swap = pltpu.make_async_remote_copy(
        src_ref=own_half,
        dst_ref=own_half,
        send_sem=hid_send,
        recv_sem=hid_recv,
        device_id={"rank": flipped(1)},
        device_id_type=MESH,
    )
    swap.start()

    def project(at, block_from):
        base = items[pl.ds(block_from, half_blocks)].reshape(half_items, model_width)
        mixed = base.astype(jnp.float32) + jnp.dot(
            hidden[pl.ds(at, half_items)], wout[...], preferred_element_type=jnp.float32
        )
        table[pl.ds(at, half_items)] = mixed.astype(jnp.bfloat16)

    def store_half(at, i):
        part = pl.ds(at, half_items)
        return pltpu.make_async_copy(table.at[part], table_hbm.at[part], store_sem.at[i])

    project(mine_at, core * half_blocks)
    store_half(mine_at, 1).start()
    swap.wait()
    project(other_at, (1 - core) * half_blocks)
    store_half(other_at, 2).start()
    store_onehot.wait()
    store_half(mine_at, 1).wait()
    store_half(other_at, 2).wait()


def item_body(pool, kv_cache, w_qu, w_out, norm_gain, cand_ids, ranker, hist_blocks, cache_slot):
    devices = lax.axis_size("rank")
    slots_here, head_count, block_len, pair_width = kv_cache.shape
    head_dim = pair_width // 2
    user_count = cache_slot.shape[0]
    rows_here, model_width = pool.shape
    item_count = devices * rows_here
    half_items = item_count // 2
    share_rows = cand_ids.shape[1] * user_count // devices
    width = head_count * head_dim
    bits = devices.bit_length() - 1
    hbm = pl.BlockSpec(memory_space=pltpu.HBM)
    dma = pltpu.SemaphoreType.DMA
    narrow, wide = jnp.bfloat16, jnp.float32
    table, onehot = pl.pallas_call(
        functools.partial(item_kernel, devices),
        out_shape=(
            jax.ShapeDtypeStruct((item_count, model_width), narrow),
            jax.ShapeDtypeStruct((share_rows, item_count), narrow),
        ),
        in_specs=[hbm] * 9,
        out_specs=(hbm, hbm),
        scratch_shapes=[
            pltpu.SMEM(cache_slot.shape, jnp.int32),
            pltpu.SMEM(ranker.shape, jnp.int32),
            pltpu.SMEM(hist_blocks.shape, jnp.int32),
            pltpu.VMEM(cand_ids.shape, jnp.int32),
            pltpu.VMEM((1, width), wide),
            pltpu.VMEM(kv_cache.shape, narrow),
            pltpu.VMEM((devices, rows_here, model_width), narrow),
            pltpu.VMEM((user_count - 1, head_count, block_len, pair_width), narrow),
            pltpu.VMEM((head_count, user_count, block_len, pair_width), narrow),
            pltpu.VMEM(w_qu.shape, narrow),
            pltpu.VMEM(w_out.shape, narrow),
            pltpu.VMEM((head_count, item_count, pair_width), narrow),
            pltpu.VMEM((head_count, item_count, head_dim), wide),
            pltpu.VMEM((head_count, half_items, head_dim), wide),
            pltpu.VMEM((head_count, half_items, head_dim), wide),
            pltpu.VMEM((head_count, half_items, head_dim), narrow),
            pltpu.VMEM((head_count, half_items, head_dim), narrow),
            pltpu.VMEM((item_count, width), narrow),
            pltpu.VMEM((item_count, model_width), narrow),
            pltpu.VMEM((share_rows, item_count), narrow),
            dma((9,)),
            dma((3,)),
            dma((bits,)),
            dma((bits,)),
            dma((head_count, user_count - 1)),
            dma((head_count, user_count - 1)),
            dma((head_count,)),
            dma((head_count,)),
            dma((head_count,)),
            dma((head_count,)),
            dma,
            dma,
        ],
        compiler_params=pltpu.CompilerParams(
            collective_id=0, has_side_effects=True, vmem_limit_bytes=62 * 1024 * 1024
        ),
    )(
        cache_slot,
        ranker,
        hist_blocks,
        cand_ids,
        norm_gain.reshape(1, width),
        pool,
        kv_cache,
        w_qu,
        w_out,
    )
    return jnp.dot(onehot, table, preferred_element_type=wide).astype(narrow)


def body(pool, kv_cache, w_qu, w_out, norm_gain, cand_ids, ranker, hist_blocks, cache_slot):
    devices = lax.axis_size("rank")
    user_count = cache_slot.shape[0]
    items_fit = pool.shape[0] * devices * devices <= cand_ids.shape[1] * user_count
    in_fours = devices == 4 * user_count and devices & (devices - 1) == 0
    chosen = item_body if items_fit and in_fours and pool.shape[0] % 16 == 0 else candidate_body
    return chosen(
        pool, kv_cache, w_qu, w_out, norm_gain, cand_ids, ranker, hist_blocks, cache_slot
    )


def solution(mesh):
    in_specs = (
        P(("groups", "rank"), None),
        P(("groups", "rank"), None, None, None),
        P(),
        P(),
        P(),
        P("groups", None),
        P(),
        P("groups"),
        P("groups", None),
    )
    out_specs = P(("groups", "rank"), None)
    return jax.shard_map(body, mesh=mesh, in_specs=in_specs, out_specs=out_specs, check_vma=False)
```

```python
import functools
import math

import jax
import jax.numpy as jnp
from jax import lax
from jax.experimental import pallas as pl
from jax.experimental.pallas import tpu as pltpu
from jax.sharding import PartitionSpec as P

norm_eps = 1e-05
MESH = pl.DeviceIdType.MESH


def partner(shard, axis, bit):
    return lax.ppermute(shard, axis, [(i, i ^ 1 << bit) for i in range(lax.axis_size(axis))])


def attend_blocks(queries, stacked, head_dim, live_steps):
    score_scale = 1.0 / math.sqrt(head_dim)

    def step_fn(running, item):
        step_index, key_block = item

        def compute(total):
            key_part = key_block[:, :head_dim]
            value_part = key_block[:, head_dim:]
            scores = lax.dot_general(
                queries, key_part, (((1,), (1,)), ((), ())), preferred_element_type=jnp.float32
            )
            weights = jax.nn.silu(scores * score_scale).astype(jnp.bfloat16)
            return total + jnp.dot(weights, value_part, preferred_element_type=jnp.float32)

        def keep_same(total):
            return total

        return (lax.cond(step_index < live_steps, compute, keep_same, running), None)

    initial = jnp.zeros((queries.shape[0], head_dim), jnp.float32)
    step_ids = jnp.arange(stacked.shape[0], dtype=jnp.int32)
    attended, unused = lax.scan(step_fn, initial, (step_ids, stacked))
    return attended


def candidate_body(pool, kv_cache, w_qu, w_out, norm_gain, cand_ids, ranker, hist_blocks, cache_slot):
    devices = lax.axis_size("rank")
    my_index = lax.axis_index("rank")
    slots_here, head_count, block_len, pair_width = kv_cache.shape
    head_dim = pair_width // 2
    user_count, most_blocks = cache_slot.shape
    model_width = pool.shape[1]
    cand_count = cand_ids.shape[1]
    slice_width = model_width // head_count
    qu_cols = 2 * head_dim
    my_group = my_index // head_count
    my_head = my_index % head_count
    bit_count = head_count.bit_length() - 1
    share_rows = cand_count // head_count
    user_range = jnp.arange(user_count, dtype=jnp.int32)
    group_match = ranker[None, :] == user_range[:, None]
    user_of_group = jnp.sum(jnp.where(group_match, user_range[None, :], 0), axis=1)
    my_user = jnp.sum(jnp.where(user_range == my_group, user_of_group, 0))
    block_range = jnp.arange(most_blocks, dtype=jnp.int32)
    live_blocks = block_range[None, :] < hist_blocks[:, None]
    owner_table = cache_slot // slots_here
    held_here = live_blocks & (owner_table == my_index)
    held_slot = jnp.sum(jnp.where(held_here, cache_slot % slots_here, 0), axis=1)
    held_flag = jnp.any(held_here, axis=1)
    slot_of_group = jnp.sum(jnp.where(group_match, held_slot[None, :], 0), axis=1)
    flag_of_group = jnp.any(group_match & held_flag[None, :], axis=1)
    outgoing = jnp.take(kv_cache, slot_of_group, axis=0)
    outgoing = jnp.where(flag_of_group[:, None, None, None], outgoing, jnp.zeros_like(outgoing))
    outgoing = outgoing.reshape(devices, block_len, pair_width)
    incoming = lax.all_to_all(outgoing, "rank", split_axis=0, concat_axis=0, tiled=True)
    my_ids = lax.dynamic_index_in_dim(cand_ids, my_user, 0, keepdims=False)
    whole_pool = lax.all_gather(pool, "rank", axis=0, tiled=True)
    cand_rows = jnp.take(whole_pool, my_ids, axis=0)
    w_head = lax.dynamic_slice_in_dim(w_qu, my_head * qu_cols, qu_cols, 1)
    head_qu = jax.nn.silu(jnp.dot(cand_rows, w_head, preferred_element_type=jnp.float32)).astype(
        jnp.bfloat16
    )
    x_part = lax.dynamic_slice_in_dim(cand_rows, my_head * slice_width, slice_width, 1)
    queries = head_qu[:, :head_dim]
    gate_part = head_qu[:, head_dim:]
    step_sources = min(16, devices)
    stacked = incoming.reshape(devices // step_sources, step_sources * block_len, pair_width)
    live_steps = stacked.shape[0]
    attended = attend_blocks(queries, stacked, head_dim, live_steps)
    total_width = head_count * head_dim
    carried = jnp.concatenate(
        [attended, gate_part.astype(jnp.float32), x_part.astype(jnp.float32)], axis=1
    )
    state = carried.reshape(head_count, share_rows, 1, carried.shape[1])
    for bit_index in reversed(range(bit_count)):
        half_count = state.shape[0] // 2
        lower_half = state[:half_count]
        upper_half = state[half_count:]
        upper_side = my_head >> bit_index & 1 == 1
        keeping = jnp.where(upper_side, upper_half, lower_half)
        giving = jnp.where(upper_side, lower_half, upper_half)
        received = partner(giving, "rank", bit_index)
        state = jnp.where(
            upper_side,
            jnp.concatenate([received, keeping], axis=2),
            jnp.concatenate([keeping, received], axis=2),
        )
    reversal = [
        sum(((source >> bit & 1) << bit_count - 1 - bit for bit in range(bit_count)))
        for source in range(head_count)
    ]
    ordered = state[0][:, jnp.array(reversal, dtype=jnp.int32), :]
    att_rows = ordered[:, :, :head_dim].reshape(share_rows, total_width)
    gate_rows = ordered[:, :, head_dim:qu_cols].reshape(share_rows, total_width)
    x_rows = ordered[:, :, qu_cols:].reshape(share_rows, model_width)
    mean_value = jnp.mean(att_rows, axis=1, keepdims=True)
    variance = jnp.mean(att_rows * att_rows, axis=1, keepdims=True) - mean_value * mean_value
    hidden = (
        (att_rows - mean_value) * lax.rsqrt(variance + norm_eps) * norm_gain[None, :] * gate_rows
    ).astype(jnp.bfloat16)
    my_rows = x_rows + jnp.dot(hidden, w_out, preferred_element_type=jnp.float32)
    return my_rows.astype(jnp.bfloat16)


def silu(x):
    half = x * 0.5
    return half + half * jnp.tanh(half)


def item_kernel(
    devices,
    slots_hbm,
    ranker_hbm,
    blocks_hbm,
    cand_hbm,
    gain_hbm,
    pool_hbm,
    kv_hbm,
    wqu_hbm,
    wout_hbm,
    out_ref,
    slots_ref,
    ranker_ref,
    blocks_ref,
    cand_ref,
    gain_ref,
    kv_ref,
    items,
    picked,
    history,
    wqu,
    wout,
    head_qu,
    partial,
    core_in,
    chip_sum,
    chip_out,
    chip_in,
    hidden,
    onehot,
    load_sem,
    pool_send,
    pool_recv,
    kv_send,
    kv_recv,
    core_send,
    core_recv,
    chip_send,
    chip_recv,
    hid_send,
    hid_recv,
):
    me = lax.axis_index("rank")
    slots_here, head_count, block_len, pair_width = kv_ref.shape
    head_dim = pair_width // 2
    user_count, most_blocks = slots_ref.shape
    rows_here, model_width = pool_hbm.shape
    item_count = devices * rows_here
    half_items = item_count // 2
    share_rows = out_ref.shape[0]
    team = devices // user_count
    bits = devices.bit_length() - 1
    score_scale = 1.0 / math.sqrt(head_dim)

    my_bits = [lax.rem(lax.div(me, 1 << j), 2) for j in range(bits)]

    def bit_of(j):
        return my_bits[j]

    def flipped(mask):
        other = me
        for j in range(bits):
            if mask >> j & 1:
                other = other + (1 << j) * (1 - 2 * bit_of(j))
        return other

    my_group = lax.div(me, team)
    share = lax.rem(me, team)
    core = bit_of(0)

    place = 0
    for j in range(bits):
        place = place + bit_of(j) * (1 << (bits - 1 - j))

    loads = [
        pltpu.make_async_copy(source, target, load_sem.at[i])
        for i, (source, target) in enumerate(
            (
                (slots_hbm, slots_ref),
                (ranker_hbm, ranker_ref),
                (blocks_hbm, blocks_ref),
                (pool_hbm, items.at[place]),
                (kv_hbm, kv_ref),
                (cand_hbm, cand_ref),
                (gain_hbm, gain_ref),
                (wqu_hbm, wqu),
                (wout_hbm, wout),
            )
        )
    ]
    for load in loads:
        load.start()
    load_slots, load_ranker, load_blocks, load_pool, load_kv = loads[:5]
    load_cand, load_gain, load_qu, load_out = loads[5:]

    barrier = pltpu.get_barrier_semaphore()
    masks = [1, 2] + [team * d for d in range(1, user_count)]
    for mask in masks:
        pl.semaphore_signal(
            barrier, inc=1, device_id={"rank": flipped(mask)}, device_id_type=MESH
        )

    load_slots.wait()
    load_ranker.wait()
    load_blocks.wait()
    first_slot = me * slots_here
    held, alive = [], []
    for u in range(user_count):
        slot, live = jnp.int32(0), jnp.int32(0)
        for b in range(most_blocks):
            entry = slots_ref[u, b]
            offset = entry - first_slot
            mine = (offset >= 0) & (offset < slots_here)
            slot = jnp.where(mine, offset, slot)
            live = jnp.where(mine & (b < blocks_ref[u]), 1, live)
        held.append(slot)
        alive.append(live)
    pl.semaphore_wait(barrier, len(masks))

    def pool_step(j):
        span = 1 << (bits - 1 - j)
        part = items.at[pl.ds(lax.div(place, span) * span, span)]
        return pltpu.make_async_remote_copy(
            src_ref=part,
            dst_ref=part,
            send_sem=pool_send.at[j],
            recv_sem=pool_recv.at[j],
            device_id={"rank": flipped(1 << j)},
            device_id_type=MESH,
        )

    def kv_copy(h, d):
        return pltpu.make_async_remote_copy(
            src_ref=picked.at[d - 1, h],
            dst_ref=history.at[h, d],
            send_sem=kv_send.at[h, d - 1],
            recv_sem=kv_recv.at[h, d - 1],
            device_id={"rank": flipped(team * d)},
            device_id_type=MESH,
        )

    far_first = range(user_count - 1, 0, -1)

    def send_head(h):
        for d in far_first:
            kv_copy(h, d).start()

    load_pool.wait()
    pool_step(bits - 1).start()

    load_kv.wait()
    for d in (*far_first, 0):
        group = lax.div(flipped(team * d), team)
        slot, live = jnp.int32(0), jnp.int32(0)
        for u in range(user_count):
            here = ranker_ref[u] == group
            slot = jnp.where(here, held[u], slot)
            live = jnp.where(here, alive[u], live)
        block = kv_ref[slot]
        block = jnp.where(live == 1, block, jnp.zeros_like(block))
        if d > 0:
            picked[d - 1] = block
        else:
            history[:, 0] = block

    waves = list(range(head_count))
    for j in range(bits - 1, 1, -1):
        pool_step(j).wait()
        pool_step(j - 1).start()
        if waves:
            send_head(waves.pop(0))
    if waves:
        send_head(waves.pop(0))

    load_cand.wait()
    first = pl.multiple_of(share * share_rows, share_rows)
    ids = jnp.zeros((1, share_rows), jnp.int32)
    for u in range(user_count):
        ids = jnp.where(ranker_ref[u] == my_group, cand_ref[pl.ds(u, 1), pl.ds(first, share_rows)], ids)
    row = lax.broadcasted_iota(jnp.int32, (rows_here, share_rows), 0)
    hits = []
    for at in range(devices):
        rank_at = sum((at >> j & 1) << bits - 1 - j for j in range(bits))
        hits.append((row + rank_at * rows_here == ids).astype(jnp.float32))
    for half in range(2):
        some = jnp.concatenate(hits[half * devices // 2 : (half + 1) * devices // 2], axis=0)
        onehot[half] = some.T.astype(jnp.bfloat16)

    half_blocks = devices // 2
    load_qu.wait()

    def project_in(at, block_from):
        some = items[pl.ds(block_from, half_blocks)].reshape(half_items, model_width)
        for h in range(head_count):
            qu = jnp.dot(
                some,
                wqu[:, h * pair_width : (h + 1) * pair_width],
                preferred_element_type=jnp.float32,
            )
            head_qu[h, pl.ds(at, half_items)] = silu(qu).astype(jnp.bfloat16)

    mine_at = pl.multiple_of(core * half_items, half_items)
    other_at = pl.multiple_of((1 - core) * half_items, half_items)

    pool_step(1).wait()
    pool_step(0).start()
    for h in waves:
        send_head(h)
    project_in(mine_at, core * half_blocks)
    pool_step(0).wait()
    project_in(other_at, (1 - core) * half_blocks)

    def core_copy(h):
        return pltpu.make_async_remote_copy(
            src_ref=partial.at[h, pl.ds(other_at, half_items)],
            dst_ref=core_in.at[h],
            send_sem=core_send.at[h],
            recv_sem=core_recv.at[h],
            device_id={"rank": flipped(1)},
            device_id_type=MESH,
        )

    def chip_copy(h):
        return pltpu.make_async_remote_copy(
            src_ref=chip_out.at[h],
            dst_ref=chip_in.at[h],
            send_sem=chip_send.at[h],
            recv_sem=chip_recv.at[h],
            device_id={"rank": flipped(2)},
            device_id_type=MESH,
        )

    def to_chip(h):
        core_copy(h).wait()
        chip_sum[h] = partial[h, pl.ds(mine_at, half_items)] + core_in[h]
        chip_out[h] = chip_sum[h].astype(jnp.bfloat16)
        chip_copy(h).start()

    for h in range(head_count):
        for d in range(1, user_count):
            kv_copy(h, d).wait()
        pairs = history[h].reshape(user_count * block_len, pair_width)
        for at in (other_at, mine_at):
            scores = lax.dot_general(
                head_qu[h, pl.ds(at, half_items), :head_dim],
                pairs[:, :head_dim],
                (((1,), (1,)), ((), ())),
                preferred_element_type=jnp.float32,
            )
            weights = silu(scores * score_scale).astype(jnp.bfloat16)
            partial[h, pl.ds(at, half_items)] = jnp.dot(
                weights, pairs[:, head_dim:], preferred_element_type=jnp.float32
            )
            if at is other_at:
                core_copy(h).start()
        if h > 0:
            to_chip(h - 1)
    to_chip(head_count - 1)

    load_gain.wait()
    load_out.wait()
    width = head_count * head_dim
    attended, mean, square = [], 0.0, 0.0
    for h in range(head_count):
        chip_copy(h).wait()
        one = chip_sum[h] + chip_in[h].astype(jnp.float32)
        mean = mean + jnp.sum(one, axis=1, keepdims=True)
        square = square + jnp.sum(one * one, axis=1, keepdims=True)
        attended.append(one)
    mean = mean / width
    square = square / width
    scale = lax.rsqrt(square - mean * mean + norm_eps)
    for h in range(head_count):
        columns = slice(h * head_dim, (h + 1) * head_dim)
        gate = head_qu[h, pl.ds(mine_at, half_items), head_dim:].astype(jnp.float32)
        normed = (attended[h] - mean) * scale * gain_ref[:, columns] * gate
        hidden[pl.ds(mine_at, half_items), columns] = normed.astype(jnp.bfloat16)

    own_half = hidden.at[pl.ds(mine_at, half_items)]
    swap = pltpu.make_async_remote_copy(
        src_ref=own_half,
        dst_ref=own_half,
        send_sem=hid_send,
        recv_sem=hid_recv,
        device_id={"rank": flipped(1)},
        device_id_type=MESH,
    )
    swap.start()

    def select(at, half):
        base = items[pl.ds(half * half_blocks, half_blocks)].reshape(half_items, model_width)
        mixed = base.astype(jnp.float32) + jnp.dot(
            hidden[pl.ds(at, half_items)], wout[...], preferred_element_type=jnp.float32
        )
        return jnp.dot(
            onehot[half], mixed.astype(jnp.bfloat16), preferred_element_type=jnp.float32
        ).astype(jnp.bfloat16)

    out_ref[...] = select(mine_at, core)
    swap.wait()
    out_ref[...] = out_ref[...] + select(other_at, 1 - core)


def item_body(pool, kv_cache, w_qu, w_out, norm_gain, cand_ids, ranker, hist_blocks, cache_slot):
    devices = lax.axis_size("rank")
    slots_here, head_count, block_len, pair_width = kv_cache.shape
    head_dim = pair_width // 2
    user_count = cache_slot.shape[0]
    rows_here, model_width = pool.shape
    item_count = devices * rows_here
    half_items = item_count // 2
    share_rows = cand_ids.shape[1] * user_count // devices
    width = head_count * head_dim
    bits = devices.bit_length() - 1
    hbm = pl.BlockSpec(memory_space=pltpu.HBM)
    dma = pltpu.SemaphoreType.DMA
    narrow, wide = jnp.bfloat16, jnp.float32
    return pl.pallas_call(
        functools.partial(item_kernel, devices),
        out_shape=jax.ShapeDtypeStruct((share_rows, model_width), narrow),
        in_specs=[hbm] * 9,
        out_specs=pl.BlockSpec(memory_space=pltpu.VMEM),
        scratch_shapes=[
            pltpu.SMEM(cache_slot.shape, jnp.int32),
            pltpu.SMEM(ranker.shape, jnp.int32),
            pltpu.SMEM(hist_blocks.shape, jnp.int32),
            pltpu.VMEM(cand_ids.shape, jnp.int32),
            pltpu.VMEM((1, width), wide),
            pltpu.VMEM(kv_cache.shape, narrow),
            pltpu.VMEM((devices, rows_here, model_width), narrow),
            pltpu.VMEM((user_count - 1, head_count, block_len, pair_width), narrow),
            pltpu.VMEM((head_count, user_count, block_len, pair_width), narrow),
            pltpu.VMEM(w_qu.shape, narrow),
            pltpu.VMEM(w_out.shape, narrow),
            pltpu.VMEM((head_count, item_count, pair_width), narrow),
            pltpu.VMEM((head_count, item_count, head_dim), wide),
            pltpu.VMEM((head_count, half_items, head_dim), wide),
            pltpu.VMEM((head_count, half_items, head_dim), wide),
            pltpu.VMEM((head_count, half_items, head_dim), narrow),
            pltpu.VMEM((head_count, half_items, head_dim), narrow),
            pltpu.VMEM((item_count, width), narrow),
            pltpu.VMEM((2, share_rows, half_items), narrow),
            dma((9,)),
            dma((bits,)),
            dma((bits,)),
            dma((head_count, user_count - 1)),
            dma((head_count, user_count - 1)),
            dma((head_count,)),
            dma((head_count,)),
            dma((head_count,)),
            dma((head_count,)),
            dma,
            dma,
        ],
        compiler_params=pltpu.CompilerParams(
            collective_id=0, has_side_effects=True, vmem_limit_bytes=62 * 1024 * 1024
        ),
    )(
        cache_slot,
        ranker,
        hist_blocks,
        cand_ids,
        norm_gain.reshape(1, width),
        pool,
        kv_cache,
        w_qu,
        w_out,
    )


def body(pool, kv_cache, w_qu, w_out, norm_gain, cand_ids, ranker, hist_blocks, cache_slot):
    devices = lax.axis_size("rank")
    user_count = cache_slot.shape[0]
    items_fit = pool.shape[0] * devices * devices <= cand_ids.shape[1] * user_count
    in_fours = devices == 4 * user_count and devices & (devices - 1) == 0
    chosen = item_body if items_fit and in_fours and pool.shape[0] % 16 == 0 else candidate_body
    return chosen(
        pool, kv_cache, w_qu, w_out, norm_gain, cand_ids, ranker, hist_blocks, cache_slot
    )


def solution(mesh):
    in_specs = (
        P(("groups", "rank"), None),
        P(("groups", "rank"), None, None, None),
        P(),
        P(),
        P(),
        P("groups", None),
        P(),
        P("groups"),
        P("groups", None),
    )
    out_specs = P(("groups", "rank"), None)
    return jax.shard_map(body, mesh=mesh, in_specs=in_specs, out_specs=out_specs, check_vma=False)
```

```python
import functools
import math

import jax
import jax.numpy as jnp
from jax import lax
from jax.experimental import pallas as pl
from jax.experimental.pallas import tpu as pltpu
from jax.sharding import PartitionSpec as P

norm_eps = 1e-05
MESH = pl.DeviceIdType.MESH


def partner(shard, axis, bit):
    return lax.ppermute(shard, axis, [(i, i ^ 1 << bit) for i in range(lax.axis_size(axis))])


def attend_blocks(queries, stacked, head_dim, live_steps):
    score_scale = 1.0 / math.sqrt(head_dim)

    def step_fn(running, item):
        step_index, key_block = item

        def compute(total):
            key_part = key_block[:, :head_dim]
            value_part = key_block[:, head_dim:]
            scores = lax.dot_general(
                queries, key_part, (((1,), (1,)), ((), ())), preferred_element_type=jnp.float32
            )
            weights = jax.nn.silu(scores * score_scale).astype(jnp.bfloat16)
            return total + jnp.dot(weights, value_part, preferred_element_type=jnp.float32)

        def keep_same(total):
            return total

        return (lax.cond(step_index < live_steps, compute, keep_same, running), None)

    initial = jnp.zeros((queries.shape[0], head_dim), jnp.float32)
    step_ids = jnp.arange(stacked.shape[0], dtype=jnp.int32)
    attended, unused = lax.scan(step_fn, initial, (step_ids, stacked))
    return attended


def candidate_body(pool, kv_cache, w_qu, w_out, norm_gain, cand_ids, ranker, hist_blocks, cache_slot):
    devices = lax.axis_size("rank")
    my_index = lax.axis_index("rank")
    slots_here, head_count, block_len, pair_width = kv_cache.shape
    head_dim = pair_width // 2
    user_count, most_blocks = cache_slot.shape
    model_width = pool.shape[1]
    cand_count = cand_ids.shape[1]
    slice_width = model_width // head_count
    qu_cols = 2 * head_dim
    my_group = my_index // head_count
    my_head = my_index % head_count
    bit_count = head_count.bit_length() - 1
    share_rows = cand_count // head_count
    user_range = jnp.arange(user_count, dtype=jnp.int32)
    group_match = ranker[None, :] == user_range[:, None]
    user_of_group = jnp.sum(jnp.where(group_match, user_range[None, :], 0), axis=1)
    my_user = jnp.sum(jnp.where(user_range == my_group, user_of_group, 0))
    block_range = jnp.arange(most_blocks, dtype=jnp.int32)
    live_blocks = block_range[None, :] < hist_blocks[:, None]
    owner_table = cache_slot // slots_here
    held_here = live_blocks & (owner_table == my_index)
    held_slot = jnp.sum(jnp.where(held_here, cache_slot % slots_here, 0), axis=1)
    held_flag = jnp.any(held_here, axis=1)
    slot_of_group = jnp.sum(jnp.where(group_match, held_slot[None, :], 0), axis=1)
    flag_of_group = jnp.any(group_match & held_flag[None, :], axis=1)
    outgoing = jnp.take(kv_cache, slot_of_group, axis=0)
    outgoing = jnp.where(flag_of_group[:, None, None, None], outgoing, jnp.zeros_like(outgoing))
    outgoing = outgoing.reshape(devices, block_len, pair_width)
    incoming = lax.all_to_all(outgoing, "rank", split_axis=0, concat_axis=0, tiled=True)
    my_ids = lax.dynamic_index_in_dim(cand_ids, my_user, 0, keepdims=False)
    whole_pool = lax.all_gather(pool, "rank", axis=0, tiled=True)
    cand_rows = jnp.take(whole_pool, my_ids, axis=0)
    w_head = lax.dynamic_slice_in_dim(w_qu, my_head * qu_cols, qu_cols, 1)
    head_qu = jax.nn.silu(jnp.dot(cand_rows, w_head, preferred_element_type=jnp.float32)).astype(
        jnp.bfloat16
    )
    x_part = lax.dynamic_slice_in_dim(cand_rows, my_head * slice_width, slice_width, 1)
    queries = head_qu[:, :head_dim]
    gate_part = head_qu[:, head_dim:]
    step_sources = min(16, devices)
    stacked = incoming.reshape(devices // step_sources, step_sources * block_len, pair_width)
    live_steps = stacked.shape[0]
    attended = attend_blocks(queries, stacked, head_dim, live_steps)
    total_width = head_count * head_dim
    carried = jnp.concatenate(
        [attended, gate_part.astype(jnp.float32), x_part.astype(jnp.float32)], axis=1
    )
    state = carried.reshape(head_count, share_rows, 1, carried.shape[1])
    for bit_index in reversed(range(bit_count)):
        half_count = state.shape[0] // 2
        lower_half = state[:half_count]
        upper_half = state[half_count:]
        upper_side = my_head >> bit_index & 1 == 1
        keeping = jnp.where(upper_side, upper_half, lower_half)
        giving = jnp.where(upper_side, lower_half, upper_half)
        received = partner(giving, "rank", bit_index)
        state = jnp.where(
            upper_side,
            jnp.concatenate([received, keeping], axis=2),
            jnp.concatenate([keeping, received], axis=2),
        )
    reversal = [
        sum(((source >> bit & 1) << bit_count - 1 - bit for bit in range(bit_count)))
        for source in range(head_count)
    ]
    ordered = state[0][:, jnp.array(reversal, dtype=jnp.int32), :]
    att_rows = ordered[:, :, :head_dim].reshape(share_rows, total_width)
    gate_rows = ordered[:, :, head_dim:qu_cols].reshape(share_rows, total_width)
    x_rows = ordered[:, :, qu_cols:].reshape(share_rows, model_width)
    mean_value = jnp.mean(att_rows, axis=1, keepdims=True)
    variance = jnp.mean(att_rows * att_rows, axis=1, keepdims=True) - mean_value * mean_value
    hidden = (
        (att_rows - mean_value) * lax.rsqrt(variance + norm_eps) * norm_gain[None, :] * gate_rows
    ).astype(jnp.bfloat16)
    my_rows = x_rows + jnp.dot(hidden, w_out, preferred_element_type=jnp.float32)
    return my_rows.astype(jnp.bfloat16)


def silu(x):
    half = x * 0.5
    return half + half * jnp.tanh(half)


def item_kernel(
    devices,
    slots_hbm,
    ranker_hbm,
    blocks_hbm,
    cand_hbm,
    gain_hbm,
    pool_hbm,
    kv_hbm,
    wqu_hbm,
    wout_hbm,
    table_hbm,
    onehot_hbm,
    slots_ref,
    ranker_ref,
    blocks_ref,
    cand_ref,
    gain_ref,
    kv_ref,
    items,
    picked,
    history,
    wqu,
    wout,
    head_qu,
    partial,
    core_in,
    chip_sum,
    chip_out,
    chip_in,
    hidden,
    table,
    onehot,
    load_sem,
    store_sem,
    pool_send,
    pool_recv,
    kv_send,
    kv_recv,
    core_send,
    core_recv,
    chip_send,
    chip_recv,
    hid_send,
    hid_recv,
):
    me = lax.axis_index("rank")
    slots_here, head_count, block_len, pair_width = kv_ref.shape
    head_dim = pair_width // 2
    user_count, most_blocks = slots_ref.shape
    rows_here, model_width = pool_hbm.shape
    item_count = devices * rows_here
    half_items = item_count // 2
    share_rows = onehot_hbm.shape[0]
    team = devices // user_count
    bits = devices.bit_length() - 1
    score_scale = 1.0 / math.sqrt(head_dim)

    my_bits = [lax.rem(lax.div(me, 1 << j), 2) for j in range(bits)]

    def bit_of(j):
        return my_bits[j]

    def flipped(mask):
        other = me
        for j in range(bits):
            if mask >> j & 1:
                other = other + (1 << j) * (1 - 2 * bit_of(j))
        return other

    my_group = lax.div(me, team)
    share = lax.rem(me, team)
    core = bit_of(0)

    place = 0
    for j in range(bits):
        place = place + bit_of(j) * (1 << (bits - 1 - j))

    loads = [
        pltpu.make_async_copy(source, target, load_sem.at[i])
        for i, (source, target) in enumerate(
            (
                (slots_hbm, slots_ref),
                (ranker_hbm, ranker_ref),
                (blocks_hbm, blocks_ref),
                (pool_hbm, items.at[place]),
                (kv_hbm, kv_ref),
                (cand_hbm, cand_ref),
                (gain_hbm, gain_ref),
                (wqu_hbm, wqu),
                (wout_hbm, wout),
            )
        )
    ]
    for load in loads:
        load.start()
    load_slots, load_ranker, load_blocks, load_pool, load_kv = loads[:5]
    load_cand, load_gain, load_qu, load_out = loads[5:]

    barrier = pltpu.get_barrier_semaphore()
    masks = [1, 2] + [team * d for d in range(1, user_count)]
    for mask in masks:
        pl.semaphore_signal(
            barrier, inc=1, device_id={"rank": flipped(mask)}, device_id_type=MESH
        )

    load_slots.wait()
    load_ranker.wait()
    load_blocks.wait()
    first_slot = me * slots_here
    held, alive = [], []
    for u in range(user_count):
        slot, live = jnp.int32(0), jnp.int32(0)
        for b in range(most_blocks):
            entry = slots_ref[u, b]
            offset = entry - first_slot
            mine = (offset >= 0) & (offset < slots_here)
            slot = jnp.where(mine, offset, slot)
            live = jnp.where(mine & (b < blocks_ref[u]), 1, live)
        held.append(slot)
        alive.append(live)
    pl.semaphore_wait(barrier, len(masks))

    def pool_step(j):
        span = 1 << (bits - 1 - j)
        part = items.at[pl.ds(lax.div(place, span) * span, span)]
        return pltpu.make_async_remote_copy(
            src_ref=part,
            dst_ref=part,
            send_sem=pool_send.at[j],
            recv_sem=pool_recv.at[j],
            device_id={"rank": flipped(1 << j)},
            device_id_type=MESH,
        )

    def kv_copy(h, d):
        return pltpu.make_async_remote_copy(
            src_ref=picked.at[d - 1, h],
            dst_ref=history.at[h, d],
            send_sem=kv_send.at[h, d - 1],
            recv_sem=kv_recv.at[h, d - 1],
            device_id={"rank": flipped(team * d)},
            device_id_type=MESH,
        )

    far_first = range(user_count - 1, 0, -1)

    def send_head(h):
        for d in far_first:
            kv_copy(h, d).start()

    load_pool.wait()
    pool_step(bits - 1).start()

    load_kv.wait()
    for d in (*far_first, 0):
        group = lax.div(flipped(team * d), team)
        slot, live = jnp.int32(0), jnp.int32(0)
        for u in range(user_count):
            here = ranker_ref[u] == group
            slot = jnp.where(here, held[u], slot)
            live = jnp.where(here, alive[u], live)
        block = kv_ref[slot]
        block = jnp.where(live == 1, block, jnp.zeros_like(block))
        if d > 0:
            picked[d - 1] = block
            kv_copy(0, d).start()
        else:
            history[:, 0] = block

    waves = list(range(1, head_count))
    for j in range(bits - 1, 1, -1):
        pool_step(j).wait()
        pool_step(j - 1).start()
        if waves:
            send_head(waves.pop(0))

    load_cand.wait()
    first = pl.multiple_of(share * share_rows, share_rows)
    ids = jnp.zeros((1, share_rows), jnp.int32)
    for u in range(user_count):
        ids = jnp.where(ranker_ref[u] == my_group, cand_ref[pl.ds(u, 1), pl.ds(first, share_rows)], ids)
    row = lax.broadcasted_iota(jnp.int32, (rows_here, share_rows), 0)
    hits = []
    for at in range(devices):
        rank_at = sum((at >> j & 1) << bits - 1 - j for j in range(bits))
        hits.append((row + rank_at * rows_here == ids).astype(jnp.float32))
    onehot[...] = jnp.concatenate(hits, axis=0).T.astype(jnp.bfloat16)
    store_onehot = pltpu.make_async_copy(onehot, onehot_hbm, store_sem.at[0])
    store_onehot.start()

    half_blocks = devices // 2
    load_qu.wait()

    def project_in(at, block_from):
        some = items[pl.ds(block_from, half_blocks)].reshape(half_items, model_width)
        for h in range(head_count):
            qu = jnp.dot(
                some,
                wqu[:, h * pair_width : (h + 1) * pair_width],
                preferred_element_type=jnp.float32,
            )
            head_qu[h, pl.ds(at, half_items)] = silu(qu).astype(jnp.bfloat16)

    mine_at = pl.multiple_of(core * half_items, half_items)
    other_at = pl.multiple_of((1 - core) * half_items, half_items)

    pool_step(1).wait()
    pool_step(0).start()
    for h in waves:
        send_head(h)
    project_in(mine_at, core * half_blocks)
    pool_step(0).wait()
    project_in(other_at, (1 - core) * half_blocks)

    def core_copy(h):
        return pltpu.make_async_remote_copy(
            src_ref=partial.at[h, pl.ds(other_at, half_items)],
            dst_ref=core_in.at[h],
            send_sem=core_send.at[h],
            recv_sem=core_recv.at[h],
            device_id={"rank": flipped(1)},
            device_id_type=MESH,
        )

    def chip_copy(h):
        return pltpu.make_async_remote_copy(
            src_ref=chip_out.at[h],
            dst_ref=chip_in.at[h],
            send_sem=chip_send.at[h],
            recv_sem=chip_recv.at[h],
            device_id={"rank": flipped(2)},
            device_id_type=MESH,
        )

    def to_chip(h):
        core_copy(h).wait()
        chip_sum[h] = partial[h, pl.ds(mine_at, half_items)] + core_in[h]
        chip_out[h] = chip_sum[h].astype(jnp.bfloat16)
        chip_copy(h).start()

    for h in range(head_count):
        for d in range(1, user_count):
            kv_copy(h, d).wait()
        pairs = history[h].reshape(user_count * block_len, pair_width)
        for at in (other_at, mine_at):
            scores = lax.dot_general(
                head_qu[h, pl.ds(at, half_items), :head_dim],
                pairs[:, :head_dim],
                (((1,), (1,)), ((), ())),
                preferred_element_type=jnp.float32,
            )
            weights = silu(scores * score_scale).astype(jnp.bfloat16)
            partial[h, pl.ds(at, half_items)] = jnp.dot(
                weights, pairs[:, head_dim:], preferred_element_type=jnp.float32
            )
            if at is other_at:
                core_copy(h).start()
        if h > 0:
            to_chip(h - 1)
    to_chip(head_count - 1)

    load_gain.wait()
    load_out.wait()
    width = head_count * head_dim
    attended, mean, square = [], 0.0, 0.0
    for h in range(head_count):
        chip_copy(h).wait()
        one = chip_sum[h] + chip_in[h].astype(jnp.float32)
        mean = mean + jnp.sum(one, axis=1, keepdims=True)
        square = square + jnp.sum(one * one, axis=1, keepdims=True)
        attended.append(one)
    mean = mean / width
    square = square / width
    scale = lax.rsqrt(square - mean * mean + norm_eps)
    for h in range(head_count):
        columns = slice(h * head_dim, (h + 1) * head_dim)
        gate = head_qu[h, pl.ds(mine_at, half_items), head_dim:].astype(jnp.float32)
        normed = (attended[h] - mean) * scale * gain_ref[:, columns] * gate
        hidden[pl.ds(mine_at, half_items), columns] = normed.astype(jnp.bfloat16)

    own_half = hidden.at[pl.ds(mine_at, half_items)]
    swap = pltpu.make_async_remote_copy(
        src_ref=own_half,
        dst_ref=own_half,
        send_sem=hid_send,
        recv_sem=hid_recv,
        device_id={"rank": flipped(1)},
        device_id_type=MESH,
    )
    swap.start()

    def project(at, block_from):
        base = items[pl.ds(block_from, half_blocks)].reshape(half_items, model_width)
        mixed = base.astype(jnp.float32) + jnp.dot(
            hidden[pl.ds(at, half_items)], wout[...], preferred_element_type=jnp.float32
        )
        table[pl.ds(at, half_items)] = mixed.astype(jnp.bfloat16)

    def store_half(at, i):
        part = pl.ds(at, half_items)
        return pltpu.make_async_copy(table.at[part], table_hbm.at[part], store_sem.at[i])

    project(mine_at, core * half_blocks)
    store_half(mine_at, 1).start()
    swap.wait()
    project(other_at, (1 - core) * half_blocks)
    store_half(other_at, 2).start()
    store_onehot.wait()
    store_half(mine_at, 1).wait()
    store_half(other_at, 2).wait()


def select_kernel(onehot_ref, table_ref, out_ref):
    out_ref[...] = jnp.dot(
        onehot_ref[...], table_ref[...], preferred_element_type=jnp.float32
    ).astype(jnp.bfloat16)


def item_body(pool, kv_cache, w_qu, w_out, norm_gain, cand_ids, ranker, hist_blocks, cache_slot):
    devices = lax.axis_size("rank")
    slots_here, head_count, block_len, pair_width = kv_cache.shape
    head_dim = pair_width // 2
    user_count = cache_slot.shape[0]
    rows_here, model_width = pool.shape
    item_count = devices * rows_here
    half_items = item_count // 2
    share_rows = cand_ids.shape[1] * user_count // devices
    width = head_count * head_dim
    bits = devices.bit_length() - 1
    hbm = pl.BlockSpec(memory_space=pltpu.HBM)
    dma = pltpu.SemaphoreType.DMA
    narrow, wide = jnp.bfloat16, jnp.float32
    table, onehot = pl.pallas_call(
        functools.partial(item_kernel, devices),
        out_shape=(
            jax.ShapeDtypeStruct((item_count, model_width), narrow),
            jax.ShapeDtypeStruct((share_rows, item_count), narrow),
        ),
        in_specs=[hbm] * 9,
        out_specs=(hbm, hbm),
        scratch_shapes=[
            pltpu.SMEM(cache_slot.shape, jnp.int32),
            pltpu.SMEM(ranker.shape, jnp.int32),
            pltpu.SMEM(hist_blocks.shape, jnp.int32),
            pltpu.VMEM(cand_ids.shape, jnp.int32),
            pltpu.VMEM((1, width), wide),
            pltpu.VMEM(kv_cache.shape, narrow),
            pltpu.VMEM((devices, rows_here, model_width), narrow),
            pltpu.VMEM((user_count - 1, head_count, block_len, pair_width), narrow),
            pltpu.VMEM((head_count, user_count, block_len, pair_width), narrow),
            pltpu.VMEM(w_qu.shape, narrow),
            pltpu.VMEM(w_out.shape, narrow),
            pltpu.VMEM((head_count, item_count, pair_width), narrow),
            pltpu.VMEM((head_count, item_count, head_dim), wide),
            pltpu.VMEM((head_count, half_items, head_dim), wide),
            pltpu.VMEM((head_count, half_items, head_dim), wide),
            pltpu.VMEM((head_count, half_items, head_dim), narrow),
            pltpu.VMEM((head_count, half_items, head_dim), narrow),
            pltpu.VMEM((item_count, width), narrow),
            pltpu.VMEM((item_count, model_width), narrow),
            pltpu.VMEM((share_rows, item_count), narrow),
            dma((9,)),
            dma((3,)),
            dma((bits,)),
            dma((bits,)),
            dma((head_count, user_count - 1)),
            dma((head_count, user_count - 1)),
            dma((head_count,)),
            dma((head_count,)),
            dma((head_count,)),
            dma((head_count,)),
            dma,
            dma,
        ],
        compiler_params=pltpu.CompilerParams(
            collective_id=0, has_side_effects=True, vmem_limit_bytes=62 * 1024 * 1024
        ),
    )(
        cache_slot,
        ranker,
        hist_blocks,
        cand_ids,
        norm_gain.reshape(1, width),
        pool,
        kv_cache,
        w_qu,
        w_out,
    )
    row_block = share_rows // 2
    return pl.pallas_call(
        select_kernel,
        grid=(2,),
        out_shape=jax.ShapeDtypeStruct((share_rows, model_width), narrow),
        in_specs=[
            pl.BlockSpec((row_block, item_count), lambda i: (i, 0)),
            pl.BlockSpec((item_count, model_width), lambda i: (0, 0)),
        ],
        out_specs=pl.BlockSpec((row_block, model_width), lambda i: (i, 0)),
        compiler_params=pltpu.CompilerParams(vmem_limit_bytes=62 * 1024 * 1024),
    )(onehot, table)


def body(pool, kv_cache, w_qu, w_out, norm_gain, cand_ids, ranker, hist_blocks, cache_slot):
    devices = lax.axis_size("rank")
    user_count = cache_slot.shape[0]
    items_fit = pool.shape[0] * devices * devices <= cand_ids.shape[1] * user_count
    in_fours = devices == 4 * user_count and devices & (devices - 1) == 0
    chosen = item_body if items_fit and in_fours and pool.shape[0] % 16 == 0 else candidate_body
    return chosen(
        pool, kv_cache, w_qu, w_out, norm_gain, cand_ids, ranker, hist_blocks, cache_slot
    )


def solution(mesh):
    in_specs = (
        P(("groups", "rank"), None),
        P(("groups", "rank"), None, None, None),
        P(),
        P(),
        P(),
        P("groups", None),
        P(),
        P("groups"),
        P("groups", None),
    )
    out_specs = P(("groups", "rank"), None)
    return jax.shard_map(body, mesh=mesh, in_specs=in_specs, out_specs=out_specs, check_vma=False)
```

```python
import functools
import math

import jax
import jax.numpy as jnp
from jax import lax
from jax.experimental import pallas as pl
from jax.experimental.pallas import tpu as pltpu
from jax.sharding import PartitionSpec as P

norm_eps = 1e-05
MESH = pl.DeviceIdType.MESH


def partner(shard, axis, bit):
    return lax.ppermute(shard, axis, [(i, i ^ 1 << bit) for i in range(lax.axis_size(axis))])


def attend_blocks(queries, stacked, head_dim, live_steps):
    score_scale = 1.0 / math.sqrt(head_dim)

    def step_fn(running, item):
        step_index, key_block = item

        def compute(total):
            key_part = key_block[:, :head_dim]
            value_part = key_block[:, head_dim:]
            scores = lax.dot_general(
                queries, key_part, (((1,), (1,)), ((), ())), preferred_element_type=jnp.float32
            )
            weights = jax.nn.silu(scores * score_scale).astype(jnp.bfloat16)
            return total + jnp.dot(weights, value_part, preferred_element_type=jnp.float32)

        def keep_same(total):
            return total

        return (lax.cond(step_index < live_steps, compute, keep_same, running), None)

    initial = jnp.zeros((queries.shape[0], head_dim), jnp.float32)
    step_ids = jnp.arange(stacked.shape[0], dtype=jnp.int32)
    attended, unused = lax.scan(step_fn, initial, (step_ids, stacked))
    return attended


def candidate_body(pool, kv_cache, w_qu, w_out, norm_gain, cand_ids, ranker, hist_blocks, cache_slot):
    devices = lax.axis_size("rank")
    my_index = lax.axis_index("rank")
    slots_here, head_count, block_len, pair_width = kv_cache.shape
    head_dim = pair_width // 2
    user_count, most_blocks = cache_slot.shape
    model_width = pool.shape[1]
    cand_count = cand_ids.shape[1]
    slice_width = model_width // head_count
    qu_cols = 2 * head_dim
    my_group = my_index // head_count
    my_head = my_index % head_count
    bit_count = head_count.bit_length() - 1
    share_rows = cand_count // head_count
    user_range = jnp.arange(user_count, dtype=jnp.int32)
    group_match = ranker[None, :] == user_range[:, None]
    user_of_group = jnp.sum(jnp.where(group_match, user_range[None, :], 0), axis=1)
    my_user = jnp.sum(jnp.where(user_range == my_group, user_of_group, 0))
    block_range = jnp.arange(most_blocks, dtype=jnp.int32)
    live_blocks = block_range[None, :] < hist_blocks[:, None]
    owner_table = cache_slot // slots_here
    held_here = live_blocks & (owner_table == my_index)
    held_slot = jnp.sum(jnp.where(held_here, cache_slot % slots_here, 0), axis=1)
    held_flag = jnp.any(held_here, axis=1)
    slot_of_group = jnp.sum(jnp.where(group_match, held_slot[None, :], 0), axis=1)
    flag_of_group = jnp.any(group_match & held_flag[None, :], axis=1)
    outgoing = jnp.take(kv_cache, slot_of_group, axis=0)
    outgoing = jnp.where(flag_of_group[:, None, None, None], outgoing, jnp.zeros_like(outgoing))
    outgoing = outgoing.reshape(devices, block_len, pair_width)
    incoming = lax.all_to_all(outgoing, "rank", split_axis=0, concat_axis=0, tiled=True)
    my_ids = lax.dynamic_index_in_dim(cand_ids, my_user, 0, keepdims=False)
    whole_pool = lax.all_gather(pool, "rank", axis=0, tiled=True)
    cand_rows = jnp.take(whole_pool, my_ids, axis=0)
    w_head = lax.dynamic_slice_in_dim(w_qu, my_head * qu_cols, qu_cols, 1)
    head_qu = jax.nn.silu(jnp.dot(cand_rows, w_head, preferred_element_type=jnp.float32)).astype(
        jnp.bfloat16
    )
    x_part = lax.dynamic_slice_in_dim(cand_rows, my_head * slice_width, slice_width, 1)
    queries = head_qu[:, :head_dim]
    gate_part = head_qu[:, head_dim:]
    step_sources = min(16, devices)
    stacked = incoming.reshape(devices // step_sources, step_sources * block_len, pair_width)
    live_steps = stacked.shape[0]
    attended = attend_blocks(queries, stacked, head_dim, live_steps)
    total_width = head_count * head_dim
    carried = jnp.concatenate(
        [attended, gate_part.astype(jnp.float32), x_part.astype(jnp.float32)], axis=1
    )
    state = carried.reshape(head_count, share_rows, 1, carried.shape[1])
    for bit_index in reversed(range(bit_count)):
        half_count = state.shape[0] // 2
        lower_half = state[:half_count]
        upper_half = state[half_count:]
        upper_side = my_head >> bit_index & 1 == 1
        keeping = jnp.where(upper_side, upper_half, lower_half)
        giving = jnp.where(upper_side, lower_half, upper_half)
        received = partner(giving, "rank", bit_index)
        state = jnp.where(
            upper_side,
            jnp.concatenate([received, keeping], axis=2),
            jnp.concatenate([keeping, received], axis=2),
        )
    reversal = [
        sum(((source >> bit & 1) << bit_count - 1 - bit for bit in range(bit_count)))
        for source in range(head_count)
    ]
    ordered = state[0][:, jnp.array(reversal, dtype=jnp.int32), :]
    att_rows = ordered[:, :, :head_dim].reshape(share_rows, total_width)
    gate_rows = ordered[:, :, head_dim:qu_cols].reshape(share_rows, total_width)
    x_rows = ordered[:, :, qu_cols:].reshape(share_rows, model_width)
    mean_value = jnp.mean(att_rows, axis=1, keepdims=True)
    variance = jnp.mean(att_rows * att_rows, axis=1, keepdims=True) - mean_value * mean_value
    hidden = (
        (att_rows - mean_value) * lax.rsqrt(variance + norm_eps) * norm_gain[None, :] * gate_rows
    ).astype(jnp.bfloat16)
    my_rows = x_rows + jnp.dot(hidden, w_out, preferred_element_type=jnp.float32)
    return my_rows.astype(jnp.bfloat16)


def silu(x):
    half = x * 0.5
    return half + half * jnp.tanh(half)


def item_kernel(
    devices,
    slots_hbm,
    ranker_hbm,
    blocks_hbm,
    cand_hbm,
    gain_hbm,
    pool_hbm,
    kv_hbm,
    wqu_hbm,
    wout_hbm,
    table_hbm,
    onehot_hbm,
    slots_ref,
    ranker_ref,
    blocks_ref,
    cand_ref,
    gain_ref,
    kv_ref,
    items,
    picked,
    history,
    wqu,
    wout,
    head_qu,
    partial,
    core_in,
    chip_sum,
    chip_out,
    chip_in,
    hidden,
    table,
    onehot,
    load_sem,
    store_sem,
    pool_send,
    pool_recv,
    kv_send,
    kv_recv,
    core_send,
    core_recv,
    chip_send,
    chip_recv,
    hid_send,
    hid_recv,
):
    me = lax.axis_index("rank")
    slots_here, head_count, block_len, pair_width = kv_ref.shape
    head_dim = pair_width // 2
    user_count, most_blocks = slots_ref.shape
    rows_here, model_width = pool_hbm.shape
    item_count = devices * rows_here
    half_items = item_count // 2
    share_rows = onehot_hbm.shape[0]
    team = devices // user_count
    bits = devices.bit_length() - 1
    score_scale = 1.0 / math.sqrt(head_dim)

    my_bits = [lax.rem(lax.div(me, 1 << j), 2) for j in range(bits)]

    def bit_of(j):
        return my_bits[j]

    def flipped(mask):
        other = me
        for j in range(bits):
            if mask >> j & 1:
                other = other + (1 << j) * (1 - 2 * bit_of(j))
        return other

    my_group = lax.div(me, team)
    share = lax.rem(me, team)
    core = bit_of(0)

    place = 0
    for j in range(bits):
        place = place + bit_of(j) * (1 << (bits - 1 - j))

    loads = [
        pltpu.make_async_copy(source, target, load_sem.at[i])
        for i, (source, target) in enumerate(
            (
                (slots_hbm, slots_ref),
                (ranker_hbm, ranker_ref),
                (blocks_hbm, blocks_ref),
                (pool_hbm, items.at[place]),
                (kv_hbm, kv_ref),
                (cand_hbm, cand_ref),
                (gain_hbm, gain_ref),
                (wqu_hbm, wqu),
                (wout_hbm, wout),
            )
        )
    ]
    for load in loads:
        load.start()
    load_slots, load_ranker, load_blocks, load_pool, load_kv = loads[:5]
    load_cand, load_gain, load_qu, load_out = loads[5:]

    barrier = pltpu.get_barrier_semaphore()
    masks = [1, 2] + [team * d for d in range(1, user_count)]
    for mask in masks:
        pl.semaphore_signal(
            barrier, inc=1, device_id={"rank": flipped(mask)}, device_id_type=MESH
        )

    load_slots.wait()
    load_ranker.wait()
    load_blocks.wait()
    first_slot = me * slots_here
    held, alive = [], []
    for u in range(user_count):
        slot, live = jnp.int32(0), jnp.int32(0)
        for b in range(most_blocks):
            entry = slots_ref[u, b]
            offset = entry - first_slot
            mine = (offset >= 0) & (offset < slots_here)
            slot = jnp.where(mine, offset, slot)
            live = jnp.where(mine & (b < blocks_ref[u]), 1, live)
        held.append(slot)
        alive.append(live)
    pl.semaphore_wait(barrier, len(masks))

    def pool_step(j):
        span = 1 << (bits - 1 - j)
        part = items.at[pl.ds(lax.div(place, span) * span, span)]
        return pltpu.make_async_remote_copy(
            src_ref=part,
            dst_ref=part,
            send_sem=pool_send.at[j],
            recv_sem=pool_recv.at[j],
            device_id={"rank": flipped(1 << j)},
            device_id_type=MESH,
        )

    def kv_copy(h, d):
        return pltpu.make_async_remote_copy(
            src_ref=picked.at[d - 1, h],
            dst_ref=history.at[h, d],
            send_sem=kv_send.at[h, d - 1],
            recv_sem=kv_recv.at[h, d - 1],
            device_id={"rank": flipped(team * d)},
            device_id_type=MESH,
        )

    far_first = range(user_count - 1, 0, -1)

    def send_head(h):
        for d in far_first:
            kv_copy(h, d).start()

    load_pool.wait()
    pool_step(bits - 1).start()

    load_kv.wait()
    for d in (*far_first, 0):
        group = lax.div(flipped(team * d), team)
        slot, live = jnp.int32(0), jnp.int32(0)
        for u in range(user_count):
            here = ranker_ref[u] == group
            slot = jnp.where(here, held[u], slot)
            live = jnp.where(here, alive[u], live)
        block = kv_ref[slot]
        block = jnp.where(live == 1, block, jnp.zeros_like(block))
        if d > 0:
            picked[d - 1] = block
            kv_copy(0, d).start()
        else:
            history[:, 0] = block

    pool_step(bits - 1).wait()
    pool_step(bits - 2).start()
    for h in range(1, head_count):
        send_head(h)
    for j in range(bits - 2, 1, -1):
        pool_step(j).wait()
        pool_step(j - 1).start()

    load_cand.wait()
    first = pl.multiple_of(share * share_rows, share_rows)
    ids = jnp.zeros((1, share_rows), jnp.int32)
    for u in range(user_count):
        ids = jnp.where(ranker_ref[u] == my_group, cand_ref[pl.ds(u, 1), pl.ds(first, share_rows)], ids)
    row = lax.broadcasted_iota(jnp.int32, (rows_here, share_rows), 0)
    hits = []
    for at in range(devices):
        rank_at = sum((at >> j & 1) << bits - 1 - j for j in range(bits))
        hits.append((row + rank_at * rows_here == ids).astype(jnp.float32))
    onehot[...] = jnp.concatenate(hits, axis=0).T.astype(jnp.bfloat16)
    store_onehot = pltpu.make_async_copy(onehot, onehot_hbm, store_sem.at[0])
    store_onehot.start()

    half_blocks = devices // 2
    load_qu.wait()

    def project_in(at, block_from):
        some = items[pl.ds(block_from, half_blocks)].reshape(half_items, model_width)
        for h in range(head_count):
            qu = jnp.dot(
                some,
                wqu[:, h * pair_width : (h + 1) * pair_width],
                preferred_element_type=jnp.float32,
            )
            head_qu[h, pl.ds(at, half_items)] = silu(qu).astype(jnp.bfloat16)

    mine_at = pl.multiple_of(core * half_items, half_items)
    other_at = pl.multiple_of((1 - core) * half_items, half_items)

    pool_step(1).wait()
    pool_step(0).start()
    project_in(mine_at, core * half_blocks)
    pool_step(0).wait()
    project_in(other_at, (1 - core) * half_blocks)

    def core_copy(h):
        return pltpu.make_async_remote_copy(
            src_ref=partial.at[h, pl.ds(other_at, half_items)],
            dst_ref=core_in.at[h],
            send_sem=core_send.at[h],
            recv_sem=core_recv.at[h],
            device_id={"rank": flipped(1)},
            device_id_type=MESH,
        )

    def chip_copy(h):
        return pltpu.make_async_remote_copy(
            src_ref=chip_out.at[h],
            dst_ref=chip_in.at[h],
            send_sem=chip_send.at[h],
            recv_sem=chip_recv.at[h],
            device_id={"rank": flipped(2)},
            device_id_type=MESH,
        )

    def to_chip(h):
        core_copy(h).wait()
        chip_sum[h] = partial[h, pl.ds(mine_at, half_items)] + core_in[h]
        chip_out[h] = chip_sum[h].astype(jnp.bfloat16)
        chip_copy(h).start()

    for h in range(head_count):
        for d in range(1, user_count):
            kv_copy(h, d).wait()
        pairs = history[h].reshape(user_count * block_len, pair_width)
        for at in (other_at, mine_at):
            scores = lax.dot_general(
                head_qu[h, pl.ds(at, half_items), :head_dim],
                pairs[:, :head_dim],
                (((1,), (1,)), ((), ())),
                preferred_element_type=jnp.float32,
            )
            weights = silu(scores * score_scale).astype(jnp.bfloat16)
            partial[h, pl.ds(at, half_items)] = jnp.dot(
                weights, pairs[:, head_dim:], preferred_element_type=jnp.float32
            )
            if at is other_at:
                core_copy(h).start()
        if h > 0:
            to_chip(h - 1)
    to_chip(head_count - 1)

    load_gain.wait()
    load_out.wait()
    width = head_count * head_dim
    attended, mean, square = [], 0.0, 0.0
    for h in range(head_count):
        chip_copy(h).wait()
        one = chip_sum[h] + chip_in[h].astype(jnp.float32)
        mean = mean + jnp.sum(one, axis=1, keepdims=True)
        square = square + jnp.sum(one * one, axis=1, keepdims=True)
        attended.append(one)
    mean = mean / width
    square = square / width
    scale = lax.rsqrt(square - mean * mean + norm_eps)
    for h in range(head_count):
        columns = slice(h * head_dim, (h + 1) * head_dim)
        gate = head_qu[h, pl.ds(mine_at, half_items), head_dim:].astype(jnp.float32)
        normed = (attended[h] - mean) * scale * gain_ref[:, columns] * gate
        hidden[pl.ds(mine_at, half_items), columns] = normed.astype(jnp.bfloat16)

    own_half = hidden.at[pl.ds(mine_at, half_items)]
    swap = pltpu.make_async_remote_copy(
        src_ref=own_half,
        dst_ref=own_half,
        send_sem=hid_send,
        recv_sem=hid_recv,
        device_id={"rank": flipped(1)},
        device_id_type=MESH,
    )
    swap.start()

    def project(at, block_from):
        base = items[pl.ds(block_from, half_blocks)].reshape(half_items, model_width)
        mixed = base.astype(jnp.float32) + jnp.dot(
            hidden[pl.ds(at, half_items)], wout[...], preferred_element_type=jnp.float32
        )
        table[pl.ds(at, half_items)] = mixed.astype(jnp.bfloat16)

    def store_half(at, i):
        part = pl.ds(at, half_items)
        return pltpu.make_async_copy(table.at[part], table_hbm.at[part], store_sem.at[i])

    project(mine_at, core * half_blocks)
    store_half(mine_at, 1).start()
    swap.wait()
    project(other_at, (1 - core) * half_blocks)
    store_half(other_at, 2).start()
    store_onehot.wait()
    store_half(mine_at, 1).wait()
    store_half(other_at, 2).wait()


def item_body(pool, kv_cache, w_qu, w_out, norm_gain, cand_ids, ranker, hist_blocks, cache_slot):
    devices = lax.axis_size("rank")
    slots_here, head_count, block_len, pair_width = kv_cache.shape
    head_dim = pair_width // 2
    user_count = cache_slot.shape[0]
    rows_here, model_width = pool.shape
    item_count = devices * rows_here
    half_items = item_count // 2
    share_rows = cand_ids.shape[1] * user_count // devices
    width = head_count * head_dim
    bits = devices.bit_length() - 1
    hbm = pl.BlockSpec(memory_space=pltpu.HBM)
    dma = pltpu.SemaphoreType.DMA
    narrow, wide = jnp.bfloat16, jnp.float32
    table, onehot = pl.pallas_call(
        functools.partial(item_kernel, devices),
        out_shape=(
            jax.ShapeDtypeStruct((item_count, model_width), narrow),
            jax.ShapeDtypeStruct((share_rows, item_count), narrow),
        ),
        in_specs=[hbm] * 9,
        out_specs=(hbm, hbm),
        scratch_shapes=[
            pltpu.SMEM(cache_slot.shape, jnp.int32),
            pltpu.SMEM(ranker.shape, jnp.int32),
            pltpu.SMEM(hist_blocks.shape, jnp.int32),
            pltpu.VMEM(cand_ids.shape, jnp.int32),
            pltpu.VMEM((1, width), wide),
            pltpu.VMEM(kv_cache.shape, narrow),
            pltpu.VMEM((devices, rows_here, model_width), narrow),
            pltpu.VMEM((user_count - 1, head_count, block_len, pair_width), narrow),
            pltpu.VMEM((head_count, user_count, block_len, pair_width), narrow),
            pltpu.VMEM(w_qu.shape, narrow),
            pltpu.VMEM(w_out.shape, narrow),
            pltpu.VMEM((head_count, item_count, pair_width), narrow),
            pltpu.VMEM((head_count, item_count, head_dim), wide),
            pltpu.VMEM((head_count, half_items, head_dim), wide),
            pltpu.VMEM((head_count, half_items, head_dim), wide),
            pltpu.VMEM((head_count, half_items, head_dim), narrow),
            pltpu.VMEM((head_count, half_items, head_dim), narrow),
            pltpu.VMEM((item_count, width), narrow),
            pltpu.VMEM((item_count, model_width), narrow),
            pltpu.VMEM((share_rows, item_count), narrow),
            dma((9,)),
            dma((3,)),
            dma((bits,)),
            dma((bits,)),
            dma((head_count, user_count - 1)),
            dma((head_count, user_count - 1)),
            dma((head_count,)),
            dma((head_count,)),
            dma((head_count,)),
            dma((head_count,)),
            dma,
            dma,
        ],
        compiler_params=pltpu.CompilerParams(
            collective_id=0, has_side_effects=True, vmem_limit_bytes=62 * 1024 * 1024
        ),
    )(
        cache_slot,
        ranker,
        hist_blocks,
        cand_ids,
        norm_gain.reshape(1, width),
        pool,
        kv_cache,
        w_qu,
        w_out,
    )
    return jnp.dot(onehot, table, preferred_element_type=wide).astype(narrow)


def body(pool, kv_cache, w_qu, w_out, norm_gain, cand_ids, ranker, hist_blocks, cache_slot):
    devices = lax.axis_size("rank")
    user_count = cache_slot.shape[0]
    items_fit = pool.shape[0] * devices * devices <= cand_ids.shape[1] * user_count
    in_fours = devices == 4 * user_count and devices & (devices - 1) == 0
    chosen = item_body if items_fit and in_fours and pool.shape[0] % 16 == 0 else candidate_body
    return chosen(
        pool, kv_cache, w_qu, w_out, norm_gain, cand_ids, ranker, hist_blocks, cache_slot
    )


def solution(mesh):
    in_specs = (
        P(("groups", "rank"), None),
        P(("groups", "rank"), None, None, None),
        P(),
        P(),
        P(),
        P("groups", None),
        P(),
        P("groups"),
        P("groups", None),
    )
    out_specs = P(("groups", "rank"), None)
    return jax.shard_map(body, mesh=mesh, in_specs=in_specs, out_specs=out_specs, check_vma=False)
```
